256 devices in a mesh: dp: 16 (over z, core), seq: 16 (over y, x).
Axes of the slice: x: 4, y: 4, z: 8, core: 2. Of those that a mesh axis runs over, the one named last changes fastest.
Arguments:
- query_states: bfloat16 [32768, 8192], P(('dp', 'seq')), parts along dimension 0, may hold values from -140 to 140
- key_states: bfloat16 [32768, 1024], P(('dp', 'seq')), parts along dimension 0, may hold values from -7 to 7
- value_states: bfloat16 [32768, 1024], P(('dp', 'seq')), parts along dimension 0, may hold values from -6 to 6
- output_grad: bfloat16 [32768, 8192], P(('dp', 'seq')), parts along dimension 0, may hold values from -6 to 6
- document_lengths: int32 [512], P('dp'), parts along dimension 0, may hold values from 1 to 191, as said below
- document_owners: int32 [512], P('dp'), parts along dimension 0, may hold values from 0 to 15, as said below
- block_table: int32 [256, 16], P('dp'), parts along dimension 0, may hold values from 0 to 1, as said below
Outputs:
- attention_out: bfloat16 [49152, 8192], P(('dp', 'seq')), parts along dimension 0
- query_grad: bfloat16 [49152, 8192], P(('dp', 'seq')), parts along dimension 0
- key_grad: bfloat16 [49152, 1024], P(('dp', 'seq')), parts along dimension 0
- value_grad: bfloat16 [49152, 1024], P(('dp', 'seq')), parts along dimension 0
The draws below stay inside these ranges and needn't reach their ends.
There are 16 independent parts, one for each index of `dp`. The reference program is written for one: setup_inputs(seed, part) draws one part's arguments, and reference() takes and returns one part's arrays. A program takes and returns all parts, laid end to end along the dimension named above; each array names one. Nothing has to cross between parts.
Inputs may be any that keep to these rules, and one draw needn't show every extreme that they name: `document_lengths`: the lengths sum to 2048; some document has exactly 191 tokens. `document_owners`: owners do not fall along the documents; every device owns one to three consecutive documents, which hold at most 192 tokens together, exactly 192 for some owner; all tokens of device d's documents lie at positions from d * 128 - 128 // 4 to (d + 1) * 128 + 128 // 4 - 1. `block_table`: the diagonal is 1.
All inputs are finite; a program needn't handle non-finite values.
Results may differ from the reference program's by a relative error of at most 0.0051.
Values may be sent and summed in bfloat16 or wider, within the bound.
A program may use at most 128 MiB of HBM per device.

```python
import jax
import jax.numpy as jnp
from jax import lax

HEADS = 64
KV_HEADS = 8
HEAD_DIM = 128
TOK_DEV = 128
BLOCK = 128
TOKENS = 2048
CAP = 192
SLOTS = 3072
DOCS = 32
NBLK = 16


def doc_layout(key):
    owners_count = DOCS // 2
    pair_count = owners_count // 2
    quarter = TOK_DEV // 4
    middle = owners_count // 2
    key_edge, key_first, key_second, key_count = jax.random.split(key, 4)
    edge_ids = jnp.arange(owners_count + 1, dtype=jnp.int32)
    edges = jax.random.randint(key_edge, (owners_count + 1,), -quarter, quarter).astype(jnp.int32)
    edges = jnp.where((edge_ids == 0) | (edge_ids == owners_count), 0, edges)
    edges = jnp.where(edge_ids == middle, -quarter, edges)
    edges = jnp.where(edge_ids == middle + 1, quarter, edges)
    bounds = edge_ids * TOK_DEV + edges
    totals = (bounds[1:] - bounds[:-1]).astype(jnp.int32)
    owner_ids = jnp.arange(owners_count, dtype=jnp.int32)
    first_cut = jax.random.randint(key_first, (owners_count,), 1, totals - 1).astype(jnp.int32)
    first_cut = jnp.where(owner_ids == middle, 1, first_cut)
    second_cut = jax.random.randint(key_second, (owners_count,), first_cut + 1, totals).astype(jnp.int32)
    pair_ids = jnp.arange(pair_count, dtype=jnp.int32)
    first_count = jax.random.randint(key_count, (pair_count,), 1, 4).astype(jnp.int32)
    first_count = jnp.where(pair_ids == middle // 2, 2, first_count)
    counts = jnp.stack([first_count, 4 - first_count], axis=1).reshape(owners_count)
    zeros = jnp.zeros_like(totals)
    single = jnp.stack([totals, zeros, zeros], axis=1)
    double = jnp.stack([first_cut, totals - first_cut, zeros], axis=1)
    triple = jnp.stack([first_cut, second_cut - first_cut, totals - second_cut], axis=1)
    pieces = jnp.where((counts == 1)[:, None], single, jnp.where((counts == 2)[:, None], double, triple))
    first_pieces = pieces[0::2]
    second_pieces = pieces[1::2]
    places = jnp.arange(4, dtype=jnp.int32)[None, :]
    from_first = places < first_count[:, None]
    first_index = jnp.clip(places, 0, 2) + jnp.zeros((pair_count, 1), jnp.int32)
    second_index = jnp.clip(places - first_count[:, None], 0, 2)
    lengths = jnp.where(from_first, jnp.take_along_axis(first_pieces, first_index, axis=1), jnp.take_along_axis(second_pieces, second_index, axis=1))
    owners = jnp.where(from_first, 2 * pair_ids[:, None], 2 * pair_ids[:, None] + 1)
    return (lengths.reshape(DOCS).astype(jnp.int32), owners.reshape(DOCS).astype(jnp.int32))


def key_base(key):
    base_key = jax.random.fold_in(key, 101)
    return jnp.clip(jax.random.normal(base_key, (TOKENS, KV_HEADS * HEAD_DIM), jnp.float32), -6.0, 6.0)


def draw_document_lengths(key, part):
    return doc_layout(key)[0]


def draw_document_owners(key, part):
    return doc_layout(key)[1]


def draw_block_table(key, part):
    key = jax.random.fold_in(key, 5)
    random_bits = jax.random.randint(key, (NBLK, NBLK), 0, 2).astype(jnp.int32)
    return jnp.maximum(random_bits, jnp.eye(NBLK, dtype=jnp.int32))


def draw_key_states(key, part):
    base = key_base(key)
    return base.astype(jnp.bfloat16)


def draw_query_states(key, part):
    key = jax.random.fold_in(key, 7)
    drawn = jnp.clip(jax.random.normal(key, (TOKENS, HEADS * HEAD_DIM), jnp.float32), -6.0, 6.0)
    return drawn.astype(jnp.bfloat16)


def block_scale(stream_key, shape, cuts, smallest, top_value):
    loudness = 1.0
    for dim, parts in cuts:
        heights = jax.random.uniform(jax.random.fold_in(jax.random.fold_in(stream_key, 6), dim), (parts,), jnp.float32, smallest / len(cuts), top_value / len(cuts))
        loudness = loudness * jnp.repeat(jnp.exp(heights), shape[dim] // parts).reshape((-1,) + (1,) * (len(shape) - 1 - dim))
    return loudness


def normal_values(stream_key, extent, scale, reach, cuts=(), held_as=jnp.bfloat16):
    entries = scale * jax.random.normal(stream_key, extent, jnp.float32)
    if cuts:
        entries = entries * block_scale(stream_key, extent, cuts, -0.22, 0.18)
    return jnp.clip(entries, -reach, reach).astype(held_as)


def setup_inputs(seed: int = 0, part: int = 0) -> dict:
    splits = jax.random.split(jax.random.key(seed), 8)
    part_keys = jax.random.split(jax.random.fold_in(splits[7], part), 8)
    query_states = draw_query_states(jax.random.fold_in(jax.random.fold_in(splits[7], part), 71), part)
    key_states = draw_key_states(jax.random.fold_in(jax.random.fold_in(splits[7], part), 71), part)
    value_states = normal_values(part_keys[2], (TOKENS, KV_HEADS * HEAD_DIM), 1.0, 6.0, ((0, 16),))
    output_grad = normal_values(part_keys[3], (TOKENS, HEADS * HEAD_DIM), 1.0, 6.0, ((0, 16),))
    document_lengths = draw_document_lengths(jax.random.fold_in(jax.random.fold_in(splits[7], part), 71), part)
    document_owners = draw_document_owners(jax.random.fold_in(jax.random.fold_in(splits[7], part), 71), part)
    block_table = draw_block_table(jax.random.fold_in(jax.random.fold_in(splits[7], part), 71), part)
    return dict(query_states=query_states, key_states=key_states, value_states=value_states, output_grad=output_grad, document_lengths=document_lengths, document_owners=document_owners, block_table=block_table)


def slot_layout(document_lengths, document_owners):
    doc_count = document_lengths.shape[0]
    starts = jnp.cumsum(document_lengths) - document_lengths
    position = jnp.arange(TOKENS, dtype=jnp.int32)
    inside = (position[:, None] >= starts[None, :]).astype(jnp.int32)
    doc_ids = jnp.sum(inside, axis=1) - 1
    numbers = jnp.arange(doc_count, dtype=jnp.int32)
    shared = (document_owners[:, None] == document_owners[None, :]) & (numbers[None, :] < numbers[:, None])
    offsets = jnp.sum(jnp.where(shared, document_lengths[None, :], 0), axis=1)
    doc_slot = document_owners * CAP + offsets - starts
    picked = doc_ids[:, None] == numbers[None, :]
    token_slot = jnp.sum(jnp.where(picked, doc_slot[None, :], 0), axis=1) + position
    return doc_ids.astype(jnp.int32), token_slot.astype(jnp.int32)


def head_pass(operands, allowed):
    query_rows, key_rows, value_rows, grad_rows = operands
    inv_root = HEAD_DIM ** -0.5
    scores = jnp.dot(query_rows, key_rows.T, preferred_element_type=jnp.float32) * inv_root
    scores = jnp.where(allowed, scores, -jnp.inf)
    highest = jnp.max(scores, axis=1, keepdims=True)
    raised = jnp.exp(scores - highest)
    summed = jnp.sum(raised, axis=1, keepdims=True)
    prob_full = raised / summed
    prob_half = prob_full.astype(jnp.bfloat16)
    output_rows = jnp.dot(prob_half, value_rows, preferred_element_type=jnp.float32).astype(jnp.bfloat16)
    prob_grad = jnp.dot(grad_rows, value_rows.T, preferred_element_type=jnp.float32)
    row_delta = jnp.sum(prob_full * prob_grad, axis=1, keepdims=True)
    score_grad = (prob_full * (prob_grad - row_delta)).astype(jnp.bfloat16)
    query_grad = (jnp.dot(score_grad, key_rows, preferred_element_type=jnp.float32) * inv_root).astype(jnp.bfloat16)
    key_grad = jnp.dot(score_grad.T, query_rows, preferred_element_type=jnp.float32) * inv_root
    value_grad = jnp.dot(prob_half.T, grad_rows, preferred_element_type=jnp.float32)
    return output_rows, query_grad, key_grad, value_grad


def reference(query_states, key_states, value_states, output_grad, document_lengths, document_owners, block_table):
    doc_ids, token_slot = slot_layout(document_lengths, document_owners)
    position = jnp.arange(TOKENS, dtype=jnp.int32)
    blocks = position // BLOCK
    table_rows = block_table[blocks[:, None], blocks[None, :]]
    allowed = (doc_ids[:, None] == doc_ids[None, :]) & (position[None, :] <= position[:, None]) & (table_rows == 1)
    group_size = HEADS // KV_HEADS
    query_heads = query_states.reshape(TOKENS, HEADS, HEAD_DIM).transpose(1, 0, 2)
    grad_heads = output_grad.reshape(TOKENS, HEADS, HEAD_DIM).transpose(1, 0, 2)
    key_heads = jnp.repeat(key_states.reshape(TOKENS, KV_HEADS, HEAD_DIM).transpose(1, 0, 2), group_size, axis=0)
    value_heads = jnp.repeat(value_states.reshape(TOKENS, KV_HEADS, HEAD_DIM).transpose(1, 0, 2), group_size, axis=0)
    outputs, query_grads, key_parts, value_parts = lax.map(lambda operands: head_pass(operands, allowed), (query_heads, key_heads, value_heads, grad_heads))
    out_rows = outputs.transpose(1, 0, 2).reshape(TOKENS, HEADS * HEAD_DIM)
    qgrad_rows = query_grads.transpose(1, 0, 2).reshape(TOKENS, HEADS * HEAD_DIM)
    kgrad_rows = key_parts.reshape(KV_HEADS, group_size, TOKENS, HEAD_DIM).sum(axis=1).transpose(1, 0, 2).reshape(TOKENS, KV_HEADS * HEAD_DIM).astype(jnp.bfloat16)
    vgrad_rows = value_parts.reshape(KV_HEADS, group_size, TOKENS, HEAD_DIM).sum(axis=1).transpose(1, 0, 2).reshape(TOKENS, KV_HEADS * HEAD_DIM).astype(jnp.bfloat16)

    def to_slots(rows):
        return jnp.zeros((SLOTS, rows.shape[1]), rows.dtype).at[token_slot].set(rows)

    return to_slots(out_rows), to_slots(qgrad_rows), to_slots(kgrad_rows), to_slots(vgrad_rows)
```

```python
import functools

import jax
import jax.numpy as jnp
from jax import lax
from jax.experimental import pallas as pl
from jax.experimental.pallas import tpu as pltpu
from jax.sharding import PartitionSpec as P

HEADS = 64
KV_HEADS = 8
HEAD_DIM = 128
BLOCK = 128
CAP = 192
HALO = 32
TOK = 128
WIN = TOK + 2 * HALO
GROUP = HEADS // KV_HEADS
GCOLS = GROUP * HEAD_DIM
QB = 64
NB = WIN // QB
CHUNK_HEADS = 4
CW = CHUNK_HEADS * QB
TALL = CAP + 2 * HALO
INV_ROOT = HEAD_DIM**-0.5
LOG2E = 1.4426950408889634
FAR = -1e30
EARLY = 0
MESH = pl.DeviceIdType.MESH
BF16 = jnp.bfloat16
F32 = jnp.float32


def dot(a, b, dims):
    return lax.dot_general(a, b, (dims, ((), ())), preferred_element_type=F32)


def clear(tall_refs):
    for ref in tall_refs:
        tail = ref.shape[:-2] + (TALL - WIN, HEAD_DIM)
        ref[..., WIN:TALL, :] = jnp.zeros(tail, F32)


def prepare(me, devices, len_ref, own_ref, table_ref, bias, owned, tall_refs):
    docs = len_ref.shape[0]
    base = me * TOK - HALO
    key_pos = base + lax.broadcasted_iota(jnp.int32, (WIN, 128), 0)
    lane = lax.broadcasted_iota(jnp.int32, (8, CW), 1) % QB
    query_pos = [base + b * QB + lane for b in range(NB)]

    def one(n, carry):
        start, first, count, key_doc, query_doc = carry
        length = len_ref[n]
        owner = own_ref[n]
        key_doc = key_doc + jnp.where(key_pos >= start, 1, 0)
        query_doc = tuple(
            d + jnp.where(p >= start, 1, 0) for d, p in zip(query_doc, query_pos)
        )
        first = first + jnp.where(owner < me, length, 0)
        count = count + jnp.where(owner == me, length, 0)
        return (start + length, first, count, key_doc, query_doc)

    zero = jnp.int32(0)
    _, first, count, key_doc, query_doc = lax.fori_loop(
        0,
        docs,
        one,
        (
            zero,
            zero,
            zero,
            jnp.zeros((WIN, 128), jnp.int32),
            tuple(jnp.zeros((8, CW), jnp.int32) for _ in range(NB)),
        ),
    )
    before = jnp.maximum(me - 1, 0)
    after = jnp.minimum(me + 1, devices - 1)
    own_before = table_ref[me, before]
    after_own = table_ref[after, me]
    after_before = table_ref[after, before]
    key_pos2 = jnp.concatenate([key_pos] * (CW // 128), axis=1)
    key_doc2 = jnp.concatenate([key_doc] * (CW // 128), axis=1)
    for b in range(NB):
        rows = (b + 1) * QB
        kp, kd = key_pos2[:rows], key_doc2[:rows]
        qp, qd = query_pos[b][:1], query_doc[b][:1]
        key_block = (kp + BLOCK) // BLOCK - me
        query_block = (qp + BLOCK) // BLOCK - me
        linked = jnp.where(
            query_block == 1,
            jnp.where(key_block == 0, own_before, 1),
            jnp.where(
                query_block == 2,
                jnp.where(key_block == 0, after_before, jnp.where(key_block == 1, after_own, 1)),
                1,
            ),
        )
        allowed = (kd == qd) & (kp <= qp) & (linked == 1)
        bias[b, 0:rows, :] = jnp.where(allowed, 0.0, FAR)
        inside = (query_pos[b] >= first) & (query_pos[b] < first + count)
        owned[b] = jnp.where(inside, 1.0, 0.0)
    clear(tall_refs)
    return first - base


def group_pass(q, g, k, v, bias, owned, out_tall, dq_tall, dk_tall, dv_tall):
    for b in reversed(range(NB)):
        rows = (b + 1) * QB
        keys, values = k[0:rows, :], v[0:rows, :]
        dk = dv = None
        for c in range(GROUP // CHUNK_HEADS):
            heads = range(c * CHUNK_HEADS, (c + 1) * CHUNK_HEADS)
            span = slice(b * QB, (b + 1) * QB)
            qs = jnp.concatenate([q[span, h * HEAD_DIM : (h + 1) * HEAD_DIM] for h in heads], axis=0)
            gs = jnp.concatenate([g[span, h * HEAD_DIM : (h + 1) * HEAD_DIM] for h in heads], axis=0)
            scores = dot(keys, qs, ((1,), (1,))) * (INV_ROOT * LOG2E) + bias[b, 0:rows, :]
            highest = jnp.max(scores, axis=0, keepdims=True)
            raised = jnp.exp2(scores - highest)
            total = jnp.sum(raised, axis=0, keepdims=True)
            prob = raised * (owned[b, 0:1, :] / total)
            half = prob.astype(BF16)
            prob_grad = dot(values, gs, ((1,), (1,)))
            delta = jnp.sum(prob * prob_grad, axis=0, keepdims=True)
            score_grad = (prob * (prob_grad - delta)).astype(BF16)
            out = dot(half, values, ((0,), (0,)))
            dq = dot(score_grad, keys, ((0,), (0,))) * INV_ROOT
            for i, h in enumerate(heads):
                out_tall[h, span, :] = out[i * QB : (i + 1) * QB]
                dq_tall[h, span, :] = dq[i * QB : (i + 1) * QB]
            dk_part = dot(score_grad, qs, ((1,), (0,)))
            dv_part = dot(half, gs, ((1,), (0,)))
            dk = dk_part if dk is None else dk + dk_part
            dv = dv_part if dv is None else dv + dv_part
        if b == NB - 1:
            dk_tall[0:rows, :] = dk
            dv_tall[0:rows, :] = dv
        else:
            dk_tall[0:rows, :] += dk
            dv_tall[0:rows, :] += dv


def shifted(shift, out_tall, dq_tall, dk_tall, dv_tall, out, dq, dk, dv):
    rows = pl.ds(shift, CAP)
    for h in range(GROUP):
        cols = slice(h * HEAD_DIM, (h + 1) * HEAD_DIM)
        out[:, cols] = out_tall[h, rows, :].astype(BF16)
        dq[:, cols] = dq_tall[h, rows, :].astype(BF16)
    dk[...] = (dk_tall[rows, :] * INV_ROOT).astype(BF16)
    dv[...] = dv_tall[rows, :].astype(BF16)


def windows(groups):
    return [(groups, WIN, GCOLS)] * 2 + [(groups, WIN, HEAD_DIM)] * 2


def tall_scratch():
    return [
        pltpu.VMEM((GROUP, TALL, HEAD_DIM), F32),
        pltpu.VMEM((GROUP, TALL, HEAD_DIM), F32),
        pltpu.VMEM((TALL, HEAD_DIM), F32),
        pltpu.VMEM((TALL, HEAD_DIM), F32),
    ]


def wide(g):
    return pl.ds(pl.multiple_of(g * GCOLS, GCOLS), GCOLS)


def thin(g):
    return pl.ds(pl.multiple_of(g * HEAD_DIM, HEAD_DIM), HEAD_DIM)


COLUMNS = (wide, wide, thin, thin)


def exchange_kernel(devices, early, *refs):
    q, g, k, v, lens, owners, table = refs[:7]
    late_windows = refs[7:11]
    bias, owned = refs[11:13]
    rest = refs[13:-3]
    done, near = (rest[:4], rest[4:8]) if early else ((), ())
    talls = rest[-4:]
    send, recv, load = refs[-3:]
    dp = lax.axis_index("dp")
    me = lax.axis_index("seq")
    right, left = lax.rem(me + 1, devices), lax.rem(me + devices - 1, devices)
    sources = (q, g, k, v)

    def window(n, a):
        if isinstance(n, int) and n >= early:
            return late_windows[a].at[n - early]
        return near[a].at[n]

    def hop(n, a, side):
        rows = pl.ds(TOK - HALO, HALO) if side == 0 else pl.ds(0, HALO)
        there = pl.ds(0, HALO) if side == 0 else pl.ds(HALO + TOK, HALO)
        return pltpu.make_async_remote_copy(
            src_ref=sources[a].at[rows, COLUMNS[a](n)],
            dst_ref=window(n, a).at[there, :],
            send_sem=send.at[n, a, side],
            recv_sem=recv.at[n, a, side],
            device_id=(dp, right if side == 0 else left),
            device_id_type=MESH,
        )

    def own(n, a):
        return pltpu.make_async_copy(
            sources[a].at[:, COLUMNS[a](n)], window(n, a).at[pl.ds(HALO, TOK), :], load.at[n, a]
        )

    barrier = pltpu.get_barrier_semaphore()
    for neighbour in (left, right):
        pl.semaphore_signal(barrier, inc=1, device_id=(dp, neighbour), device_id_type=MESH)
    pl.semaphore_wait(barrier, 2)
    for n in range(KV_HEADS):
        for a in (2, 3, 0, 1):
            for side in range(2):
                hop(n, a, side).start()
    for n in range(KV_HEADS):
        for a in range(4):
            own(n, a).start()
    shift = prepare(me, devices, lens, owners, table, bias, owned, talls)

    def step(n, carry):
        for a in range(4):
            own(n, a).wait()
            for side in range(2):
                hop(n, a, side).wait()
        group_pass(*(w.at[n] for w in near), bias, owned, *talls)
        shifted(shift, *talls, *(d.at[n] for d in done))
        return carry

    if early:
        lax.fori_loop(0, early, step, 0)
    for n in range(early, KV_HEADS):
        for a in range(4):
            own(n, a).wait()
            for side in range(2):
                hop(n, a, side).wait()


def finish_kernel(early, *refs):
    late = KV_HEADS - early
    lens, owners = refs[:2]
    late_windows = refs[2:6]
    bias, owned = refs[6:8]
    done = refs[8:-13]
    outs = refs[-13:-9]
    stage = refs[-9:-5]
    talls = refs[-5:-1]
    store = refs[-1]
    me = lax.axis_index("seq")

    def write(n, a):
        src = done[a].at[n] if n < early else stage[a].at[n - early]
        return pltpu.make_async_copy(src, outs[a].at[:, COLUMNS[a](n)], store.at[n, a])

    for n in range(early):
        for a in range(4):
            write(n, a).start()

    def one(n, first):
        return first + jnp.where(owners[n] < me, lens[n], 0)

    shift = lax.fori_loop(0, lens.shape[0], one, jnp.int32(0)) - (me * TOK - HALO)
    clear(talls)
    for n in range(late):
        group_pass(*(w.at[n] for w in late_windows), bias, owned, *talls)
        shifted(shift, *talls, *(s.at[n] for s in stage))
        for a in range(4):
            write(early + n, a).start()
    for n in range(KV_HEADS):
        for a in range(4):
            write(n, a).wait()


def local(devices, early, q, k, v, g, lens, owners, table):
    late = KV_HEADS - early
    any_spec = pl.BlockSpec(memory_space=pl.ANY)
    smem = pl.BlockSpec(memory_space=pltpu.SMEM)
    arrays = [pltpu.with_memory_space_constraint(x, pltpu.HBM) for x in (q, g, k, v)]
    lens, owners, table = [pltpu.with_memory_space_constraint(x, pltpu.HBM) for x in (lens, owners, table)]
    results = [(CAP, GCOLS)] * 2 + [(CAP, HEAD_DIM)] * 2
    mid_shapes = (
        [pltpu.VMEM(s, BF16) for s in windows(late)]
        + [pltpu.VMEM((NB, WIN, CW), F32), pltpu.VMEM((NB, 8, CW), F32)]
        + [pltpu.VMEM((early, *s), BF16) for s in results if early]
    )
    mid = pl.pallas_call(
        functools.partial(exchange_kernel, devices, early),
        out_shape=mid_shapes,
        in_specs=[any_spec] * 4 + [smem] * 3,
        out_specs=[pl.BlockSpec(memory_space=pltpu.VMEM)] * len(mid_shapes),
        scratch_shapes=[pltpu.VMEM(s, BF16) for s in windows(early) if early]
        + tall_scratch()
        + [
            pltpu.SemaphoreType.DMA((KV_HEADS, 4, 2)),
            pltpu.SemaphoreType.DMA((KV_HEADS, 4, 2)),
            pltpu.SemaphoreType.DMA((KV_HEADS, 4)),
        ],
        compiler_params=pltpu.CompilerParams(
            collective_id=0, has_side_effects=True, vmem_limit_bytes=24 << 20
        ),
        name="exchange",
    )(*arrays, lens, owners, table)
    mid = [pltpu.with_memory_space_constraint(x, pltpu.VMEM) for x in mid]
    shapes = [(CAP, w) for w in (HEADS * HEAD_DIM,) * 2 + (KV_HEADS * HEAD_DIM,) * 2]
    return tuple(
        pl.pallas_call(
            functools.partial(finish_kernel, early),
            out_shape=[pltpu.HBM(s, BF16) for s in shapes],
            in_specs=[smem] * 2 + [pl.BlockSpec(memory_space=pltpu.VMEM)] * len(mid),
            out_specs=[any_spec] * 4,
            scratch_shapes=[pltpu.VMEM((late, *s), BF16) for s in results]
            + tall_scratch()
            + [pltpu.SemaphoreType.DMA((KV_HEADS, 4))],
            compiler_params=pltpu.CompilerParams(vmem_limit_bytes=24 << 20),
            name="finish",
        )(lens, owners, *mid)
    )


def solution(mesh):
    rows = P(("dp", "seq"), None)
    return jax.shard_map(
        functools.partial(local, mesh.shape["seq"], EARLY),
        mesh=mesh,
        in_specs=(rows, rows, rows, rows, P("dp"), P("dp"), P("dp", None)),
        out_specs=(rows, rows, rows, rows),
        check_vma=False,
    )
```

```python
import functools

import jax
import jax.numpy as jnp
from jax import lax
from jax.experimental import pallas as pl
from jax.experimental.pallas import tpu as pltpu
from jax.sharding import PartitionSpec as P

HEADS = 64
KV_HEADS = 8
HEAD_DIM = 128
BLOCK = 128
CAP = 192
HALO = 32
TOK = 128
WIN = TOK + 2 * HALO
GROUP = HEADS // KV_HEADS
GCOLS = GROUP * HEAD_DIM
QB = 64
NB = WIN // QB
CHUNK_HEADS = 4
CW = CHUNK_HEADS * QB
TALL = CAP + 2 * HALO
INV_ROOT = HEAD_DIM**-0.5
LOG2E = 1.4426950408889634
FAR = -1e30
EARLY = 7
MESH = pl.DeviceIdType.MESH
BF16 = jnp.bfloat16
F32 = jnp.float32


def dot(a, b, dims):
    return lax.dot_general(a, b, (dims, ((), ())), preferred_element_type=F32)


def clear(tall_refs):
    for ref in tall_refs:
        tail = ref.shape[:-2] + (TALL - WIN, HEAD_DIM)
        ref[..., WIN:TALL, :] = jnp.zeros(tail, F32)


def prepare(me, devices, len_ref, own_ref, table_ref, bias, owned, tall_refs):
    docs = len_ref.shape[0]
    base = me * TOK - HALO
    key_pos = base + lax.broadcasted_iota(jnp.int32, (WIN, 128), 0)
    lane = lax.broadcasted_iota(jnp.int32, (8, CW), 1) % QB
    query_pos = [base + b * QB + lane for b in range(NB)]

    def one(n, carry):
        start, first, count, key_doc, query_doc = carry
        length = len_ref[n]
        owner = own_ref[n]
        key_doc = key_doc + jnp.where(key_pos >= start, 1, 0)
        query_doc = tuple(
            d + jnp.where(p >= start, 1, 0) for d, p in zip(query_doc, query_pos)
        )
        first = first + jnp.where(owner < me, length, 0)
        count = count + jnp.where(owner == me, length, 0)
        return (start + length, first, count, key_doc, query_doc)

    zero = jnp.int32(0)
    _, first, count, key_doc, query_doc = lax.fori_loop(
        0,
        docs,
        one,
        (
            zero,
            zero,
            zero,
            jnp.zeros((WIN, 128), jnp.int32),
            tuple(jnp.zeros((8, CW), jnp.int32) for _ in range(NB)),
        ),
    )
    before = jnp.maximum(me - 1, 0)
    after = jnp.minimum(me + 1, devices - 1)
    own_before = table_ref[me, before]
    after_own = table_ref[after, me]
    after_before = table_ref[after, before]
    key_pos2 = jnp.concatenate([key_pos] * (CW // 128), axis=1)
    key_doc2 = jnp.concatenate([key_doc] * (CW // 128), axis=1)
    for b in range(NB):
        rows = (b + 1) * QB
        kp, kd = key_pos2[:rows], key_doc2[:rows]
        qp, qd = query_pos[b][:1], query_doc[b][:1]
        key_block = (kp + BLOCK) // BLOCK - me
        query_block = (qp + BLOCK) // BLOCK - me
        linked = jnp.where(
            query_block == 1,
            jnp.where(key_block == 0, own_before, 1),
            jnp.where(
                query_block == 2,
                jnp.where(key_block == 0, after_before, jnp.where(key_block == 1, after_own, 1)),
                1,
            ),
        )
        allowed = (kd == qd) & (kp <= qp) & (linked == 1)
        bias[b, 0:rows, :] = jnp.where(allowed, 0.0, FAR)
        inside = (query_pos[b] >= first) & (query_pos[b] < first + count)
        owned[b] = jnp.where(inside, 1.0, 0.0)
    clear(tall_refs)
    return jnp.clip(first - base, 0, 2 * HALO)


def group_pass(q, g, k, v, bias, owned, out_tall, dq_tall, dk_tall, dv_tall):
    for b in reversed(range(NB)):
        rows = (b + 1) * QB
        keys, values = k[0:rows, :], v[0:rows, :]
        dk = dv = None
        for c in range(GROUP // CHUNK_HEADS):
            heads = range(c * CHUNK_HEADS, (c + 1) * CHUNK_HEADS)
            span = slice(b * QB, (b + 1) * QB)
            qs = jnp.concatenate([q[span, h * HEAD_DIM : (h + 1) * HEAD_DIM] for h in heads], axis=0)
            gs = jnp.concatenate([g[span, h * HEAD_DIM : (h + 1) * HEAD_DIM] for h in heads], axis=0)
            scores = dot(keys, qs, ((1,), (1,))) * (INV_ROOT * LOG2E) + bias[b, 0:rows, :]
            highest = jnp.max(scores, axis=0, keepdims=True)
            raised = jnp.exp2(scores - highest)
            total = jnp.sum(raised, axis=0, keepdims=True)
            prob = raised * (owned[b, 0:1, :] / total)
            half = prob.astype(BF16)
            prob_grad = dot(values, gs, ((1,), (1,)))
            delta = jnp.sum(prob * prob_grad, axis=0, keepdims=True)
            score_grad = (prob * (prob_grad - delta)).astype(BF16)
            out = dot(half, values, ((0,), (0,)))
            dq = dot(score_grad, keys, ((0,), (0,))) * INV_ROOT
            for i, h in enumerate(heads):
                out_tall[h, span, :] = out[i * QB : (i + 1) * QB]
                dq_tall[h, span, :] = dq[i * QB : (i + 1) * QB]
            dk_part = dot(score_grad, qs, ((1,), (0,)))
            dv_part = dot(half, gs, ((1,), (0,)))
            dk = dk_part if dk is None else dk + dk_part
            dv = dv_part if dv is None else dv + dv_part
        if b == NB - 1:
            dk_tall[0:rows, :] = dk
            dv_tall[0:rows, :] = dv
        else:
            dk_tall[0:rows, :] += dk
            dv_tall[0:rows, :] += dv


def shifted(shift, out_tall, dq_tall, dk_tall, dv_tall, out, dq, dk, dv):
    rows = pl.ds(shift, CAP)
    for h in range(GROUP):
        cols = slice(h * HEAD_DIM, (h + 1) * HEAD_DIM)
        out[:, cols] = out_tall[h, rows, :].astype(BF16)
        dq[:, cols] = dq_tall[h, rows, :].astype(BF16)
    dk[...] = (dk_tall[rows, :] * INV_ROOT).astype(BF16)
    dv[...] = dv_tall[rows, :].astype(BF16)


def windows(groups):
    return [(groups, WIN, GCOLS)] * 2 + [(groups, WIN, HEAD_DIM)] * 2


def tall_scratch():
    return [
        pltpu.VMEM((GROUP, TALL, HEAD_DIM), F32),
        pltpu.VMEM((GROUP, TALL, HEAD_DIM), F32),
        pltpu.VMEM((TALL, HEAD_DIM), F32),
        pltpu.VMEM((TALL, HEAD_DIM), F32),
    ]


def wide(g):
    return pl.ds(pl.multiple_of(g * GCOLS, GCOLS), GCOLS)


def thin(g):
    return pl.ds(pl.multiple_of(g * HEAD_DIM, HEAD_DIM), HEAD_DIM)


COLUMNS = (wide, wide, thin, thin)


def exchange_kernel(devices, early, *refs):
    q, g, k, v, lens, owners, table = refs[:7]
    late_windows = refs[7:11]
    bias, owned = refs[11:13]
    done = refs[13:17]
    near = [refs[17 + 4 * n : 21 + 4 * n] for n in range(early)]
    talls = refs[-7:-3]
    send, recv, load = refs[-3:]
    dp = lax.axis_index("dp")
    me = lax.axis_index("seq")
    right, left = lax.rem(me + 1, devices), lax.rem(me + devices - 1, devices)
    sources = (q, g, k, v)

    def window(n, a):
        return near[n][a] if n < early else late_windows[a].at[n - early]

    def hop(n, a, side):
        rows = pl.ds(TOK - HALO, HALO) if side == 0 else pl.ds(0, HALO)
        there = pl.ds(0, HALO) if side == 0 else pl.ds(HALO + TOK, HALO)
        return pltpu.make_async_remote_copy(
            src_ref=sources[a].at[rows, COLUMNS[a](n)],
            dst_ref=window(n, a).at[there, :],
            send_sem=send.at[n, a, side],
            recv_sem=recv.at[n, a, side],
            device_id=(dp, right if side == 0 else left),
            device_id_type=MESH,
        )

    def own(n, a):
        return pltpu.make_async_copy(
            sources[a].at[:, COLUMNS[a](n)], window(n, a).at[pl.ds(HALO, TOK), :], load.at[n, a]
        )

    barrier = pltpu.get_barrier_semaphore()
    for neighbour in (left, right):
        pl.semaphore_signal(barrier, inc=1, device_id=(dp, neighbour), device_id_type=MESH)
    pl.semaphore_wait(barrier, 2)
    for n in range(KV_HEADS):
        for a in (2, 3, 0, 1):
            for side in range(2):
                hop(n, a, side).start()
    for n in range(KV_HEADS):
        for a in range(4):
            own(n, a).start()
    shift = prepare(me, devices, lens, owners, table, bias, owned, talls)

    for n in range(KV_HEADS):
        for a in range(4):
            own(n, a).wait()
            for side in range(2):
                hop(n, a, side).wait()
        if n < early:
            group_pass(*near[n], bias, owned, *talls)
            shifted(shift, *talls, *(d.at[n] for d in done))


def finish_kernel(early, *refs):
    late = KV_HEADS - early
    lens, owners = refs[:2]
    late_windows = refs[2:6]
    bias, owned = refs[6:8]
    done = refs[8:12]
    outs = refs[12:16]
    stage = refs[16:20]
    talls = refs[20:24]
    store = refs[24]
    me = lax.axis_index("seq")

    def write(n, a):
        src = done[a].at[n] if n < early else stage[a].at[n - early]
        return pltpu.make_async_copy(src, outs[a].at[:, COLUMNS[a](n)], store.at[n, a])

    for n in range(early):
        for a in range(4):
            write(n, a).start()

    def one(n, first):
        return first + jnp.where(owners[n] < me, lens[n], 0)

    shift = lax.fori_loop(0, lens.shape[0], one, jnp.int32(0)) - (me * TOK - HALO)
    shift = jnp.clip(shift, 0, 2 * HALO)
    clear(talls)
    for n in range(late):
        group_pass(*(w.at[n] for w in late_windows), bias, owned, *talls)
        shifted(shift, *talls, *(s.at[n] for s in stage))
        for a in range(4):
            write(early + n, a).start()
    for n in range(KV_HEADS):
        for a in range(4):
            write(n, a).wait()


def local(devices, early, q, k, v, g, lens, owners, table):
    late = KV_HEADS - early
    any_spec = pl.BlockSpec(memory_space=pl.ANY)
    smem = pl.BlockSpec(memory_space=pltpu.SMEM)
    arrays = [pltpu.with_memory_space_constraint(x, pltpu.HBM) for x in (q, g, k, v)]
    lens, owners, table = [pltpu.with_memory_space_constraint(x, pltpu.HBM) for x in (lens, owners, table)]
    results = [(CAP, GCOLS)] * 2 + [(CAP, HEAD_DIM)] * 2
    mid_shapes = (
        [pltpu.VMEM(s, BF16) for s in windows(late)]
        + [pltpu.VMEM((NB, WIN, CW), F32), pltpu.VMEM((NB, 8, CW), F32)]
        + [pltpu.VMEM((early, *s), BF16) for s in results]
    )
    mid = pl.pallas_call(
        functools.partial(exchange_kernel, devices, early),
        out_shape=mid_shapes,
        in_specs=[any_spec] * 4 + [smem] * 3,
        out_specs=[pl.BlockSpec(memory_space=pltpu.VMEM)] * len(mid_shapes),
        scratch_shapes=[pltpu.VMEM(s[1:], BF16) for s in windows(1) * early]
        + tall_scratch()
        + [
            pltpu.SemaphoreType.DMA((KV_HEADS, 4, 2)),
            pltpu.SemaphoreType.DMA((KV_HEADS, 4, 2)),
            pltpu.SemaphoreType.DMA((KV_HEADS, 4)),
        ],
        compiler_params=pltpu.CompilerParams(
            collective_id=0, has_side_effects=True, vmem_limit_bytes=24 << 20
        ),
        name="exchange",
    )(*arrays, lens, owners, table)
    mid = [pltpu.with_memory_space_constraint(x, pltpu.VMEM) for x in mid]
    shapes = [(CAP, w) for w in (HEADS * HEAD_DIM,) * 2 + (KV_HEADS * HEAD_DIM,) * 2]
    return tuple(
        pl.pallas_call(
            functools.partial(finish_kernel, early),
            out_shape=[pltpu.HBM(s, BF16) for s in shapes],
            in_specs=[smem] * 2 + [pl.BlockSpec(memory_space=pltpu.VMEM)] * len(mid),
            out_specs=[any_spec] * 4,
            scratch_shapes=[pltpu.VMEM((late, *s), BF16) for s in results]
            + tall_scratch()
            + [pltpu.SemaphoreType.DMA((KV_HEADS, 4))],
            compiler_params=pltpu.CompilerParams(vmem_limit_bytes=24 << 20),
            name="finish",
        )(lens, owners, *mid)
    )


def solution(mesh):
    rows = P(("dp", "seq"), None)
    return jax.shard_map(
        functools.partial(local, mesh.shape["seq"], EARLY),
        mesh=mesh,
        in_specs=(rows, rows, rows, rows, P("dp"), P("dp"), P("dp", None)),
        out_specs=(rows, rows, rows, rows),
        check_vma=False,
    )
```

```python
import functools

import jax
import jax.numpy as jnp
from jax import lax
from jax.experimental import pallas as pl
from jax.experimental.pallas import tpu as pltpu
from jax.sharding import PartitionSpec as P

HEADS = 64
KV_HEADS = 8
HEAD_DIM = 128
BLOCK = 128
CAP = 192
HALO = 32
TOK = 128
WIN = TOK + 2 * HALO
GROUP = HEADS // KV_HEADS
GCOLS = GROUP * HEAD_DIM
QB = 64
CHUNK_HEADS = 4
CW = CHUNK_HEADS * QB
OWN_BLOCKS = ((HALO + QB, QB, HALO + 2 * QB), (HALO, QB, HALO + QB))
HALO_BLOCKS = ((HALO + TOK, HALO, WIN), (0, HALO, HALO))
BLOCKS = OWN_BLOCKS + HALO_BLOCKS
TALL = CAP + 2 * HALO
INV_ROOT = HEAD_DIM**-0.5
LOG2E = 1.4426950408889634
FAR = -1e30
MESH = pl.DeviceIdType.MESH
BF16 = jnp.bfloat16
F32 = jnp.float32


def dot(a, b, dims):
    return lax.dot_general(a, b, (dims, ((), ())), preferred_element_type=F32)


def clear(tall_refs):
    for ref in tall_refs:
        tail = ref.shape[:-2] + (TALL - WIN, HEAD_DIM)
        ref[..., WIN:TALL, :] = jnp.zeros(tail, F32)


def prepare(me, devices, len_ref, own_ref, table_ref, biases, owned):
    docs = len_ref.shape[0]
    base = me * TOK - HALO
    key_pos = base + lax.broadcasted_iota(jnp.int32, (WIN, 128), 0)
    lane = lax.broadcasted_iota(jnp.int32, (8, CW), 1)
    query_pos = [base + first + lane % count for first, count, _ in BLOCKS]

    def one(n, carry):
        start, first, count, key_doc, query_doc = carry
        length = len_ref[n]
        owner = own_ref[n]
        key_doc = key_doc + jnp.where(key_pos >= start, 1, 0)
        query_doc = tuple(
            d + jnp.where(p >= start, 1, 0) for d, p in zip(query_doc, query_pos)
        )
        first = first + jnp.where(owner < me, length, 0)
        count = count + jnp.where(owner == me, length, 0)
        return (start + length, first, count, key_doc, query_doc)

    zero = jnp.int32(0)
    _, first, count, key_doc, query_doc = lax.fori_loop(
        0,
        docs,
        one,
        (
            zero,
            zero,
            zero,
            jnp.zeros((WIN, 128), jnp.int32),
            tuple(jnp.zeros((8, CW), jnp.int32) for _ in BLOCKS),
        ),
    )
    before = jnp.maximum(me - 1, 0)
    after = jnp.minimum(me + 1, devices - 1)
    own_before = table_ref[me, before]
    after_own = table_ref[after, me]
    after_before = table_ref[after, before]
    key_pos2 = jnp.concatenate([key_pos] * (CW // 128), axis=1)
    key_doc2 = jnp.concatenate([key_doc] * (CW // 128), axis=1)
    for b, (_, _, rows) in enumerate(BLOCKS):
        kp, kd = key_pos2[:rows], key_doc2[:rows]
        qp, qd = query_pos[b][:1], query_doc[b][:1]
        key_block = (kp + BLOCK) // BLOCK - me
        query_block = (qp + BLOCK) // BLOCK - me
        linked = jnp.where(
            query_block == 1,
            jnp.where(key_block == 0, own_before, 1),
            jnp.where(
                query_block == 2,
                jnp.where(key_block == 0, after_before, jnp.where(key_block == 1, after_own, 1)),
                1,
            ),
        )
        allowed = (kd == qd) & (kp <= qp) & (linked == 1)
        biases[b][...] = jnp.where(allowed, 0.0, FAR)
        inside = (query_pos[b] >= first) & (query_pos[b] < first + count)
        owned[b] = jnp.where(inside, 1.0, 0.0)
    return jnp.clip(first - base, 0, 2 * HALO)


def block_pass(b, heads, q, g, k, v, bias, owned, out_tall, dq_tall):
    first, count, rows = BLOCKS[b]
    span = slice(first, first + count)
    width = count * len(heads)
    keys, values = k[0:rows, :], v[0:rows, :]
    qs = jnp.concatenate([q[span, h * HEAD_DIM : (h + 1) * HEAD_DIM] for h in heads], axis=0)
    gs = jnp.concatenate([g[span, h * HEAD_DIM : (h + 1) * HEAD_DIM] for h in heads], axis=0)
    scores = dot(keys, qs, ((1,), (1,))) * (INV_ROOT * LOG2E) + bias[:, 0:width]
    highest = jnp.max(scores, axis=0, keepdims=True)
    raised = jnp.exp2(scores - highest)
    total = jnp.sum(raised, axis=0, keepdims=True)
    prob = raised * (owned[b, 0:1, 0:width] / total)
    half = prob.astype(BF16)
    prob_grad = dot(values, gs, ((1,), (1,)))
    delta = jnp.sum(prob * prob_grad, axis=0, keepdims=True)
    score_grad = (prob * (prob_grad - delta)).astype(BF16)
    out = dot(half, values, ((0,), (0,)))
    dq = dot(score_grad, keys, ((0,), (0,))) * INV_ROOT
    for i, h in enumerate(heads):
        out_tall[h, span, :] = out[i * count : (i + 1) * count]
        dq_tall[h, span, :] = dq[i * count : (i + 1) * count]
    return dot(score_grad, qs, ((1,), (0,))), dot(half, gs, ((1,), (0,)))


def own_pass(fresh, q, g, k, v, biases, owned, out_tall, dq_tall, dk_tall, dv_tall):
    count = q.shape[1] // HEAD_DIM
    for b, (_, _, rows) in enumerate(OWN_BLOCKS):
        dk = dv = None
        for c in range(count // CHUNK_HEADS):
            heads = range(c * CHUNK_HEADS, (c + 1) * CHUNK_HEADS)
            dk_part, dv_part = block_pass(b, heads, q, g, k, v, biases[b], owned, out_tall, dq_tall)
            dk = dk_part if dk is None else dk + dk_part
            dv = dv_part if dv is None else dv + dv_part
        if fresh and b == 0:
            dk_tall[0:rows, :] = dk
            dv_tall[0:rows, :] = dv
        else:
            dk_tall[0:rows, :] += dk
            dv_tall[0:rows, :] += dv


def halo_pass(fresh, q, g, k, v, biases, owned, out_tall, dq_tall, dk_tall, dv_tall):
    heads = range(q.shape[1] // HEAD_DIM)
    for b, (_, _, rows) in enumerate(BLOCKS):
        if b < len(OWN_BLOCKS):
            continue
        dk, dv = block_pass(b, heads, q, g, k, v, biases[b], owned, out_tall, dq_tall)
        old = min(rows, HALO + TOK) if fresh else rows
        dk_tall[0:old, :] += dk[0:old]
        dv_tall[0:old, :] += dv[0:old]
        if old < rows:
            dk_tall[old:rows, :] = dk[old:rows]
            dv_tall[old:rows, :] = dv[old:rows]


def shift_queries(shift, out_tall, dq_tall, out, dq):
    rows = pl.ds(shift, CAP)
    for h in range(out.shape[1] // HEAD_DIM):
        cols = slice(h * HEAD_DIM, (h + 1) * HEAD_DIM)
        out[:, cols] = out_tall[h, rows, :].astype(BF16)
        dq[:, cols] = dq_tall[h, rows, :].astype(BF16)


def shift_keys(shift, dk_tall, dv_tall, dk, dv):
    rows = pl.ds(shift, CAP)
    dk[...] = (dk_tall[rows, :] * INV_ROOT).astype(BF16)
    dv[...] = dv_tall[rows, :].astype(BF16)


AHEAD = 2
UNITS = [(n, 0, GROUP) for n in range(KV_HEADS - 1)] + [
    (KV_HEADS - 1, 0, GROUP // 2),
    (KV_HEADS - 1, GROUP // 2, GROUP // 2),
]
LAST_COLS = UNITS[-1][2] * HEAD_DIM
EARLY_COLS = HEADS * HEAD_DIM - LAST_COLS
KV_COLS = KV_HEADS * HEAD_DIM
EARLY_KV = KV_COLS - HEAD_DIM


def unit_cols(u):
    n, first, count = UNITS[u]
    return pl.ds(n * GCOLS + first * HEAD_DIM, count * HEAD_DIM)


def kv_cols(n):
    return pl.ds(n * HEAD_DIM, HEAD_DIM)


def exchange_kernel(devices, *refs):
    q, g, k, v, lens, owners, table = refs[:7]
    kw, vw = refs[7:9]
    halo_biases = refs[9:11]
    owned, last_q, last_g, done_o, done_q, done_k, done_v = refs[11:18]
    last_talls, last_kv_talls = refs[18:20], refs[20:22]
    biases = refs[22:24] + halo_biases
    early = len(UNITS) - 1
    at = 24
    near = [refs[at + 2 * u : at + 2 + 2 * u] for u in range(early)] + [(last_q, last_g)]
    at += 2 * early
    talls = [refs[at + 2 * u : at + 2 + 2 * u] for u in range(early)] + [last_talls]
    at += 2 * early
    kv_talls = [refs[at + 2 * n : at + 2 + 2 * n] for n in range(KV_HEADS - 1)] + [last_kv_talls]
    send, recv, load, kv_send, kv_recv, kv_load = refs[-6:]
    dp = lax.axis_index("dp")
    me = lax.axis_index("seq")
    has = (me < devices - 1, me > 0)
    peer = (jnp.minimum(me + 1, devices - 1), jnp.maximum(me - 1, 0))

    def hop(src, cols, dst, side, sems):
        rows = pl.ds(TOK - HALO, HALO) if side == 0 else pl.ds(0, HALO)
        there = pl.ds(0, HALO) if side == 0 else pl.ds(HALO + TOK, HALO)
        return pltpu.make_async_remote_copy(
            src_ref=src.at[rows, cols],
            dst_ref=dst.at[there, :],
            send_sem=sems[0],
            recv_sem=sems[1],
            device_id=(dp, peer[side]),
            device_id_type=MESH,
        )

    def own(src, cols, dst, sem):
        return pltpu.make_async_copy(src.at[:, cols], dst.at[pl.ds(HALO, TOK), :], sem)

    every = pl.ds(0, KV_COLS)
    kv = ((k, kw), (v, vw))
    kv_hops = [
        [hop(src, every, dst, side, (kv_send.at[a, side], kv_recv.at[a, side])) for a, (src, dst) in enumerate(kv)]
        for side in range(2)
    ]
    kv_own = [own(src, every, dst, kv_load.at[a]) for a, (src, dst) in enumerate(kv)]
    hops = [
        [
            [
                hop(src, unit_cols(u), near[u][a], side, (send.at[u, a, side], recv.at[u, a, side]))
                for a, src in enumerate((q, g))
            ]
            for side in range(2)
        ]
        for u in range(len(UNITS))
    ]
    owns = [
        [own(src, unit_cols(u), near[u][a], load.at[u, a]) for a, src in enumerate((q, g))]
        for u in range(len(UNITS))
    ]

    barrier = pltpu.get_barrier_semaphore()
    for side in range(2):

        @pl.when(has[side])
        def _():
            pl.semaphore_signal(barrier, inc=1, device_id=(dp, peer[side]), device_id_type=MESH)

    peers = jnp.where(has[0], 1, 0) + jnp.where(has[1], 1, 0)
    pl.semaphore_wait(barrier, peers)
    for part in [kv_hops] + hops:
        for side in range(2):

            @pl.when(has[side])
            def _():
                for copy in part[side]:
                    copy.start()

    for part in [kv_own] + owns:
        for copy in part:
            copy.start()
    buffers = [ref for pair in near for ref in pair] + [kw, vw]
    for side in range(2):

        @pl.when(jnp.logical_not(has[1 - side]))
        def _():
            for ref in buffers:
                rows = pl.ds(0, HALO) if side == 0 else pl.ds(HALO + TOK, HALO)
                ref[rows, :] = jnp.zeros((HALO, ref.shape[1]), BF16)

    shift = prepare(me, devices, lens, owners, table, biases, owned)
    for pair in talls + kv_talls:
        clear(pair)

    def arrive(part):
        for side in range(2):

            @pl.when(has[side])
            def _():
                for copy in part[side]:
                    copy.wait_send()

            @pl.when(has[1 - side])
            def _():
                for copy in part[side]:
                    copy.wait_recv()

    def operands(u):
        n, first, count = UNITS[u]
        return (
            first == 0, *near[u], kw.at[:, kv_cols(n)], vw.at[:, kv_cols(n)], biases, owned,
            *talls[u], *kv_talls[n],
        )

    def own_rows(u):
        for copy in owns[u]:
            copy.wait()
        own_pass(*operands(u))

    for copy in kv_own:
        copy.wait()
    arrive(kv_hops)
    for u in range(AHEAD):
        own_rows(u)
    for u, (n, first, count) in enumerate(UNITS):
        if u + AHEAD < len(UNITS):
            own_rows(u + AHEAD)
        arrive(hops[u])
        if u == early:
            break
        halo_pass(*operands(u))
        shift_queries(shift, *talls[u], done_o.at[:, unit_cols(u)], done_q.at[:, unit_cols(u)])
        if first + count == GROUP:
            shift_keys(shift, *kv_talls[n], done_k.at[:, kv_cols(n)], done_v.at[:, kv_cols(n)])


def finish_kernel(lens, owners, kw, vw, bias_after, bias_before, owned, last_q, last_g, done_o, done_q, done_k, done_v,
                  out_part, dq_part, dk_part, dv_part, out, dq, dk, dv, stage_o, stage_q, stage_k, stage_v,
                  out_tall, dq_tall, dk_tall, dv_tall, flush, store):
    me = lax.axis_index("seq")
    pieces = 4
    width = EARLY_COLS // pieces
    moves = []
    for p in range(pieces):
        cols = pl.ds(p * width, width)
        moves.append(pltpu.make_async_copy(done_o.at[:, cols], out.at[:, cols], flush.at[p, 0]))
        moves.append(pltpu.make_async_copy(done_q.at[:, cols], dq.at[:, cols], flush.at[p, 1]))
    cols = pl.ds(0, EARLY_KV)
    moves.append(pltpu.make_async_copy(done_k, dk.at[:, cols], flush.at[pieces, 0]))
    moves.append(pltpu.make_async_copy(done_v, dv.at[:, cols], flush.at[pieces, 1]))
    for move in moves:
        move.start()

    def one(n, first):
        return first + jnp.where(owners[n] < me, lens[n], 0)

    shift = lax.fori_loop(0, lens.shape[0], one, jnp.int32(0)) - (me * TOK - HALO)
    shift = jnp.clip(shift, 0, 2 * HALO)
    middle = slice(HALO, HALO + TOK)
    for ref, part in ((out_tall, out_part), (dq_tall, dq_part)):
        ref[:, middle, :] = part[:, middle, :]
    clear((out_tall, dq_tall))
    dk_tall[...] = dk_part[...]
    dv_tall[...] = dv_part[...]
    n = KV_HEADS - 1
    halo_pass(
        False, last_q, last_g, kw.at[:, kv_cols(n)], vw.at[:, kv_cols(n)], (None, None, bias_after, bias_before), owned,
        out_tall, dq_tall, dk_tall, dv_tall,
    )
    shift_queries(shift, out_tall, dq_tall, stage_o, stage_q)
    shift_keys(shift, dk_tall, dv_tall, stage_k, stage_v)
    cols = pl.ds(EARLY_COLS, LAST_COLS)
    rest = [
        pltpu.make_async_copy(stage_o, out.at[:, cols], store.at[0]),
        pltpu.make_async_copy(stage_q, dq.at[:, cols], store.at[1]),
        pltpu.make_async_copy(stage_k, dk.at[:, kv_cols(n)], store.at[2]),
        pltpu.make_async_copy(stage_v, dv.at[:, kv_cols(n)], store.at[3]),
    ]
    for move in rest:
        move.start()
    for move in moves + rest:
        move.wait()


def local(devices, q, k, v, g, lens, owners, table):
    any_spec = pl.BlockSpec(memory_space=pl.ANY)
    vmem = pl.BlockSpec(memory_space=pltpu.VMEM)
    smem = pl.BlockSpec(memory_space=pltpu.SMEM)
    q, k, v, g, lens, owners, table = [
        pltpu.with_memory_space_constraint(x, pltpu.HBM) for x in (q, k, v, g, lens, owners, table)
    ]
    def tall(count):
        return pltpu.VMEM((count, TALL, HEAD_DIM), F32)

    def bias(b):
        return pltpu.VMEM((BLOCKS[b][2], CW), F32)

    kv_tall = pltpu.VMEM((TALL, HEAD_DIM), F32)
    units = len(UNITS)
    last_talls = [tall(UNITS[-1][2])] * 2 + [kv_tall] * 2
    mid_shapes = (
        [pltpu.VMEM((WIN, KV_COLS), BF16)] * 2
        + [bias(2), bias(3), pltpu.VMEM((len(BLOCKS), 8, CW), F32)]
        + [pltpu.VMEM((WIN, LAST_COLS), BF16)] * 2
        + [pltpu.VMEM((CAP, EARLY_COLS), BF16)] * 2
        + [pltpu.VMEM((CAP, EARLY_KV), BF16)] * 2
        + last_talls
    )
    near = [pltpu.VMEM((WIN, count * HEAD_DIM), BF16) for _, _, count in UNITS[:-1] for _ in range(2)]
    talls = [tall(count) for _, _, count in UNITS[:-1] for _ in range(2)]
    dma = pltpu.SemaphoreType.DMA
    mid = pl.pallas_call(
        functools.partial(exchange_kernel, devices),
        out_shape=mid_shapes,
        in_specs=[any_spec] * 4 + [smem] * 3,
        out_specs=[vmem] * len(mid_shapes),
        scratch_shapes=[bias(0), bias(1)]
        + near
        + talls
        + [kv_tall] * (2 * (KV_HEADS - 1))
        + [dma((units, 2, 2)), dma((units, 2, 2)), dma((units, 2)), dma((2, 2)), dma((2, 2)), dma((2,))],
        compiler_params=pltpu.CompilerParams(
            collective_id=0, has_side_effects=True, vmem_limit_bytes=40 << 20
        ),
        name="exchange",
    )(q, g, k, v, lens, owners, table)
    mid = [pltpu.with_memory_space_constraint(x, pltpu.VMEM) for x in mid]
    shapes = [(CAP, w) for w in (HEADS * HEAD_DIM,) * 2 + (KV_COLS,) * 2]
    return tuple(
        pl.pallas_call(
            finish_kernel,
            out_shape=[pltpu.HBM(s, BF16) for s in shapes],
            in_specs=[smem] * 2 + [vmem] * len(mid),
            out_specs=[any_spec] * 4,
            scratch_shapes=[pltpu.VMEM((CAP, LAST_COLS), BF16)] * 2
            + [pltpu.VMEM((CAP, HEAD_DIM), BF16)] * 2
            + last_talls
            + [dma((5, 2)), dma((4,))],
            compiler_params=pltpu.CompilerParams(vmem_limit_bytes=24 << 20),
            name="finish",
        )(lens, owners, *mid)
    )


def solution(mesh):
    rows = P(("dp", "seq"), None)
    return jax.shard_map(
        functools.partial(local, mesh.shape["seq"]),
        mesh=mesh,
        in_specs=(rows, rows, rows, rows, P("dp"), P("dp"), P("dp", None)),
        out_specs=(rows, rows, rows, rows),
        check_vma=False,
    )
```

```python
import functools

import jax
import jax.numpy as jnp
from jax import lax
from jax.experimental import pallas as pl
from jax.experimental.pallas import tpu as pltpu
from jax.sharding import PartitionSpec as P

HEADS = 64
KV_HEADS = 8
HEAD_DIM = 128
BLOCK = 128
CAP = 192
HALO = 32
TOK = 128
WIN = TOK + 2 * HALO
GROUP = HEADS // KV_HEADS
GCOLS = GROUP * HEAD_DIM
QB = 64
CHUNK_HEADS = 4
CW = CHUNK_HEADS * QB
OWN_BLOCKS = ((HALO + QB, QB, 0, HALO + 2 * QB), (HALO, QB, 0, HALO + QB))
AFTER = 2
LENT = 3
BLOCKS = OWN_BLOCKS + ((HALO + TOK, HALO, 0, WIN), (TOK, HALO, TOK, HALO + TOK))
ROW = 4
TALL = CAP + 2 * HALO
INV_ROOT = HEAD_DIM**-0.5
LOG2E = 1.4426950408889634
FAR = -1e30
MESH = pl.DeviceIdType.MESH
BF16 = jnp.bfloat16
F32 = jnp.float32


def dot(a, b, dims):
    return lax.dot_general(a, b, (dims, ((), ())), preferred_element_type=F32)


def clear(tall_refs):
    for ref in tall_refs:
        tail = ref.shape[:-2] + (TALL - WIN, HEAD_DIM)
        ref[..., WIN:TALL, :] = jnp.zeros(tail, F32)


def prepare(me, devices, len_ref, own_ref, table_ref, biases, owned):
    docs = len_ref.shape[0]
    base = me * TOK - HALO
    key_pos = base + lax.broadcasted_iota(jnp.int32, (WIN, 128), 0)
    lane = lax.broadcasted_iota(jnp.int32, (8, CW), 1)
    query_pos = [base + first + lane % count for first, count, _, _ in BLOCKS]

    def one(n, carry):
        start, first, count, lent, key_doc, query_doc = carry
        length = len_ref[n]
        owner = own_ref[n]
        key_doc = key_doc + jnp.where(key_pos >= start, 1, 0)
        query_doc = tuple(
            d + jnp.where(p >= start, 1, 0) for d, p in zip(query_doc, query_pos)
        )
        first = first + jnp.where(owner < me, length, 0)
        count = count + jnp.where(owner == me, length, 0)
        lent = lent + jnp.where(owner == me + 1, length, 0)
        return (start + length, first, count, lent, key_doc, query_doc)

    zero = jnp.int32(0)
    _, first, count, lent, key_doc, query_doc = lax.fori_loop(
        0,
        docs,
        one,
        (
            zero,
            zero,
            zero,
            zero,
            jnp.zeros((WIN, 128), jnp.int32),
            tuple(jnp.zeros((8, CW), jnp.int32) for _ in BLOCKS),
        ),
    )
    before = jnp.maximum(me - 1, 0)
    after = jnp.minimum(me + 1, devices - 1)
    own_before = table_ref[me, before]
    after_own = table_ref[after, me]
    after_before = table_ref[after, before]
    key_pos2 = jnp.concatenate([key_pos] * (CW // 128), axis=1)
    key_doc2 = jnp.concatenate([key_doc] * (CW // 128), axis=1)
    for b, (_, _, low, high) in enumerate(BLOCKS):
        kp, kd = key_pos2[low:high], key_doc2[low:high]
        qp, qd = query_pos[b][:1], query_doc[b][:1]
        key_block = (kp + BLOCK) // BLOCK - me
        query_block = (qp + BLOCK) // BLOCK - me
        linked = jnp.where(
            query_block == 1,
            jnp.where(key_block == 0, own_before, 1),
            jnp.where(
                query_block == 2,
                jnp.where(key_block == 0, after_before, jnp.where(key_block == 1, after_own, 1)),
                1,
            ),
        )
        allowed = (kd == qd) & (kp <= qp) & (linked == 1)
        biases[b][...] = jnp.where(allowed, 0.0, FAR)
        begin, size = (first + count, lent) if b == LENT else (first, count)
        inside = (query_pos[b] >= begin) & (query_pos[b] < begin + size)
        owned[b] = jnp.where(inside, 1.0, 0.0)
    return jnp.clip(first - base, 0, 2 * HALO)


def head_rows(ref, n):
    cols = slice(n * HEAD_DIM, (n + 1) * HEAD_DIM)
    return lambda low, high: ref[low:high, cols]


def scores_of(job, q, g, k, v):
    b, heads = job
    first, count, low, high = BLOCKS[b]
    span = slice(first, first + count)
    qs = jnp.concatenate([q[span, h * HEAD_DIM : (h + 1) * HEAD_DIM] for h in heads], axis=0)
    gs = jnp.concatenate([g[span, h * HEAD_DIM : (h + 1) * HEAD_DIM] for h in heads], axis=0)
    return dot(k(low, high), qs, ((1,), (1,))), dot(v(low, high), gs, ((1,), (1,))), qs, gs


def softmax_of(job, scores, prob_grad, biases, owned):
    b, heads = job
    width = BLOCKS[b][1] * len(heads)
    scores = scores * (INV_ROOT * LOG2E) + biases[b][:, 0:width]
    highest = jnp.max(scores, axis=0, keepdims=True)
    raised = jnp.exp2(scores - highest)
    total = jnp.sum(raised, axis=0, keepdims=True)
    prob = raised * (owned[b, 0:1, 0:width] / total)
    delta = jnp.sum(prob * prob_grad, axis=0, keepdims=True)
    return prob.astype(BF16), (prob * (prob_grad - delta)).astype(BF16)


def query_rows(half, score_grad, first, count, heads, keys, values, out_tall, dq_tall):
    span = slice(first, first + count)
    out = dot(half, values, ((0,), (0,)))
    dq = dot(score_grad, keys, ((0,), (0,))) * INV_ROOT
    for i, h in enumerate(heads):
        out_tall[h, span, :] = out[i * count : (i + 1) * count]
        dq_tall[h, span, :] = dq[i * count : (i + 1) * count]


def key_terms(half, score_grad, qs, gs):
    return dot(score_grad, qs, ((1,), (0,))), dot(half, gs, ((1,), (0,)))


def run_jobs(jobs, fresh_rows, q, g, k, v, biases, owned, out_tall, dq_tall, dk_tall, dv_tall):
    first = [scores_of(job, q, g, k, v) for job in jobs]
    second = [softmax_of(job, f[0], f[1], biases, owned) for job, f in zip(jobs, first)]
    sums = {}
    for (b, heads), (_, _, qs, gs), (half, score_grad) in zip(jobs, first, second):
        start, count, low, high = BLOCKS[b]
        query_rows(half, score_grad, start, count, heads, k(low, high), v(low, high), out_tall, dq_tall)
        dk, dv = key_terms(half, score_grad, qs, gs)
        old = sums.get(b)
        sums[b] = (dk, dv) if old is None else (old[0] + dk, old[1] + dv)
    for b, (dk, dv) in sums.items():
        rows = BLOCKS[b][3]
        old = min(rows, fresh_rows)
        if old:
            dk_tall[0:old, :] += dk[0:old]
            dv_tall[0:old, :] += dv[0:old]
        if old < rows:
            dk_tall[old:rows, :] = dk[old:rows]
            dv_tall[old:rows, :] = dv[old:rows]
        fresh_rows = max(fresh_rows, rows)


def own_pass(fresh, q, *rest):
    count = q.shape[1] // HEAD_DIM
    jobs = [
        (b, range(c, c + CHUNK_HEADS))
        for b in range(len(OWN_BLOCKS))
        for c in range(0, count, CHUNK_HEADS)
    ]
    run_jobs(jobs, 0 if fresh else WIN, q, *rest)


def lend_pass(q, g, k, v, biases, owned, parcel):
    job = (LENT, range(q.shape[1] // HEAD_DIM))
    scores, prob_grad, qs, gs = scores_of(job, q, g, k, v)
    half, score_grad = softmax_of(job, scores, prob_grad, biases, owned)
    width = half.shape[1]
    parcel[:, 0:width] = half
    parcel[:, width : 2 * width] = score_grad
    dk, dv = key_terms(half, score_grad, qs, gs)
    parcel[:, 2 * width : 2 * width + HEAD_DIM] = dk.astype(BF16)
    parcel[:, 2 * width + HEAD_DIM : 2 * width + 2 * HEAD_DIM] = dv.astype(BF16)


def halo_pass(fresh, q, g, k, v, biases, owned, out_tall, dq_tall, dk_tall, dv_tall, parcel):
    heads = range(q.shape[1] // HEAD_DIM)
    width = HALO * len(heads)
    query_rows(
        parcel[:, 0:width], parcel[:, width : 2 * width], 0, HALO, heads, k(0, HALO), v(0, HALO), out_tall, dq_tall
    )
    run_jobs(
        [(AFTER, heads)], HALO + TOK if fresh else WIN, q, g, k, v, biases, owned, out_tall, dq_tall, dk_tall, dv_tall
    )
    dk_tall[0:HALO, :] += parcel[:, 2 * width : 2 * width + HEAD_DIM].astype(F32)
    dv_tall[0:HALO, :] += parcel[:, 2 * width + HEAD_DIM : 2 * width + 2 * HEAD_DIM].astype(F32)


def shift_queries(shift, out_tall, dq_tall, out, dq):
    rows = pl.ds(shift, CAP)
    for h in range(out.shape[1] // HEAD_DIM):
        cols = slice(h * HEAD_DIM, (h + 1) * HEAD_DIM)
        out[:, cols] = out_tall[h, rows, :].astype(BF16)
        dq[:, cols] = dq_tall[h, rows, :].astype(BF16)


def shift_keys(shift, dk_tall, dv_tall, dk, dv):
    rows = pl.ds(shift, CAP)
    dk[...] = (dk_tall[rows, :] * INV_ROOT).astype(BF16)
    dv[...] = dv_tall[rows, :].astype(BF16)


AHEAD = 7
LEND_CUTS = (4, 6)
RELAY_AT = (3, 6)
RELAYED = 6
UNITS = [(n, 0, GROUP) for n in range(KV_HEADS - 1)] + [
    (KV_HEADS - 1, 0, GROUP // 2),
    (KV_HEADS - 1, GROUP // 2, GROUP // 2),
]
LAST_COLS = UNITS[-1][2] * HEAD_DIM
EARLY_COLS = HEADS * HEAD_DIM - LAST_COLS
KV_COLS = KV_HEADS * HEAD_DIM
EARLY_KV = KV_COLS - HEAD_DIM


def unit_cols(u):
    n, first, count = UNITS[u]
    return pl.ds(n * GCOLS + first * HEAD_DIM, count * HEAD_DIM)


def kv_cols(n):
    return pl.ds(n * HEAD_DIM, HEAD_DIM)


def exchange_kernel(devices, *refs):
    refs = list(refs)

    def take(count):
        taken = refs[:count]
        del refs[:count]
        return taken

    def pairs(count):
        return [take(2) for _ in range(count)]

    units = len(UNITS)
    early = units - 1
    q, g, k, v, lens, owners, table = take(7)
    kw, vw, bias_after, owned, last_q, last_g, done_o, done_q, done_k, done_v = take(10)
    last_talls, last_kv_talls = pairs(2)
    last_lent = take(1)
    biases = take(2) + [bias_after] + take(1)
    near = pairs(early) + [(last_q, last_g)]
    talls = pairs(early) + [last_talls]
    kv_talls = pairs(KV_HEADS - 1) + [last_kv_talls]
    lent = take(early) + last_lent
    lend = take(units)
    relay = pairs(2)
    send, recv, load, kv_send, kv_recv, kv_load, lend_send, lend_recv, relay_send, relay_recv = take(10)
    dp = lax.axis_index("dp")
    me = lax.axis_index("seq")
    x = lax.rem(me, ROW)
    has = (me < devices - 1, me > 0)
    peer = (jnp.minimum(me + 1, devices - 1), jnp.maximum(me - 1, 0))
    near_row = me - x + lax.rem(x + 1, ROW)
    above = (x == 0) | ((x == 1) & (me < devices - ROW))
    below = (x == ROW - 1) | ((x == 0) & (me > 0))
    relay_to = jnp.maximum(jnp.where(x == 0, me - 3, near_row), 0)
    relayed = (me != 0, me != devices - 3, me != devices - 2, me != devices - 1)

    def remote(src, dst, target, send_sem, recv_sem):
        return pltpu.make_async_remote_copy(
            src_ref=src, dst_ref=dst, send_sem=send_sem, recv_sem=recv_sem, device_id=(dp, target), device_id_type=MESH
        )

    def hop(src, cols, dst, side, sems):
        rows = pl.ds(TOK - HALO, HALO) if side == 0 else pl.ds(0, HALO)
        there = pl.ds(0, HALO) if side == 0 else pl.ds(HALO + TOK, HALO)
        return remote(src.at[rows, cols], dst.at[there, :], peer[side], *sems)

    def own(src, cols, dst, sem):
        return pltpu.make_async_copy(src.at[:, cols], dst.at[pl.ds(HALO, TOK), :], sem)

    every = pl.ds(0, KV_COLS)
    kv = ((k, kw), (v, vw))
    kv_hops = [
        [hop(src, every, dst, side, (kv_send.at[a, side], kv_recv.at[a, side])) for a, (src, dst) in enumerate(kv)]
        for side in range(2)
    ]
    kv_own = [own(src, every, dst, kv_load.at[a]) for a, (src, dst) in enumerate(kv)]
    hops = [
        [
            hop(src, unit_cols(u), near[u][a], 1, (send.at[u, a], recv.at[u, a]))
            for a, src in enumerate((q, g))
            if u != RELAYED
        ]
        for u in range(units)
    ]
    lends = [
        [remote(lend[u], lent[u], peer[0], lend_send.at[u], lend_recv.at[u])] for u in range(units)
    ]
    after = pl.ds(HALO + TOK, HALO)
    relays = [
        [
            remote(src.at[pl.ds(0, HALO), unit_cols(RELAYED)], relay[0][a], relay_to, relay_send.at[0, a], relay_recv.at[0, a])
            for a, src in enumerate((q, g))
        ],
        [remote(relay[0][a], relay[1][a], near_row, relay_send.at[1, a], relay_recv.at[1, a]) for a in range(2)],
        [
            remote(relay[1][a], near[RELAYED][a].at[after, :], near_row, relay_send.at[2, a], relay_recv.at[2, a])
            for a in range(2)
        ],
    ]
    owns = [
        [own(src, unit_cols(u), near[u][a], load.at[u, a]) for a, src in enumerate((q, g))]
        for u in range(units)
    ]

    barrier = pltpu.get_barrier_semaphore()
    greet = ((has[0], peer[0]), (has[1], peer[1]), (above, jnp.minimum(me + 3, devices - 1)), (below, jnp.maximum(me - 3, 0)))
    peers = jnp.int32(0)
    for meets, other in greet:
        peers = peers + jnp.where(meets, 1, 0)

        @pl.when(meets)
        def _():
            pl.semaphore_signal(barrier, inc=1, device_id=(dp, other), device_id_type=MESH)

    pl.semaphore_wait(barrier, peers)

    def start(copies):
        for copy in copies:
            copy.start()

    def arrive(copies, sends, receives):
        @pl.when(sends)
        def _():
            for copy in copies:
                copy.wait_send()

        @pl.when(receives)
        def _():
            for copy in copies:
                copy.wait_recv()

    for side in (0, 1):

        @pl.when(has[side])
        def _():
            start(kv_hops[side])

    @pl.when(relayed[0])
    def _():
        start(relays[0])

    for u in range(units):
        if u != RELAYED:

            @pl.when(has[1])
            def _():
                start(hops[u])

    start(kv_own)
    for copies in owns:
        start(copies)

    def fill(ref, rows):
        ref[rows, :] = jnp.zeros((HALO, ref.shape[1]), ref.dtype)

    @pl.when(me == 0)
    def _():
        for ref in lent + [kw, vw]:
            fill(ref, pl.ds(0, HALO))

    @pl.when(me == devices - 1)
    def _():
        for ref in [r for pair in near for r in pair] + [kw, vw]:
            fill(ref, after)

    shift = prepare(me, devices, lens, owners, table, biases, owned)
    for pair in talls + kv_talls:
        clear(pair)

    def columns(u):
        return head_rows(kw, UNITS[u][0]), head_rows(vw, UNITS[u][0])

    def operands(u):
        n, first, _ = UNITS[u]
        return (first == 0, *near[u], *columns(u), biases, owned, *talls[u], *kv_talls[n])

    def lend_rows(u):
        for copy in owns[u]:
            copy.wait()
        lend_pass(*near[u], *columns(u), biases, owned, lend[u])

    def lend_out(first, last):
        @pl.when(has[0])
        def _():
            for copies in lends[first:last]:
                start(copies)

    for copy in kv_own:
        copy.wait()
    for u in range(units):
        lend_rows(u)
    lend_out(0, LEND_CUTS[0])
    arrive(kv_hops[0], has[0], has[1])
    for u in range(RELAY_AT[0]):
        own_pass(*operands(u))
    arrive(relays[0], relayed[0], relayed[1])

    @pl.when(relayed[1])
    def _():
        start(relays[1])

    lend_out(*LEND_CUTS[0:2])
    for u in range(*RELAY_AT):
        own_pass(*operands(u))
    arrive(relays[1], relayed[1], relayed[2])

    @pl.when(relayed[2])
    def _():
        start(relays[2])

    lend_out(LEND_CUTS[1], units)
    for u in range(RELAY_AT[1], AHEAD):
        own_pass(*operands(u))
    arrive(kv_hops[1], has[1], has[0])
    for u, (n, first, count) in enumerate(UNITS):
        if u + AHEAD < units:
            own_pass(*operands(u + AHEAD))
        if u == RELAYED:
            arrive(relays[2], relayed[2], relayed[3])
        else:
            arrive(hops[u], has[1], has[0])
        arrive(lends[u], has[0], has[1])
        if u == early:
            break
        halo_pass(*operands(u), lent[u])
        shift_queries(shift, *talls[u], done_o.at[:, unit_cols(u)], done_q.at[:, unit_cols(u)])
        if first + count == GROUP:
            shift_keys(shift, *kv_talls[n], done_k.at[:, kv_cols(n)], done_v.at[:, kv_cols(n)])


def finish_kernel(lens, owners, kw, vw, bias_after, owned, last_q, last_g, done_o, done_q, done_k, done_v,
                  out_part, dq_part, dk_part, dv_part, parcel, out, dq, dk, dv, stage_o, stage_q, stage_k, stage_v,
                  out_tall, dq_tall, dk_tall, dv_tall, flush, store):
    me = lax.axis_index("seq")
    pieces = 4
    width = EARLY_COLS // pieces
    moves = []
    for p in range(pieces):
        cols = pl.ds(p * width, width)
        moves.append(pltpu.make_async_copy(done_o.at[:, cols], out.at[:, cols], flush.at[p, 0]))
        moves.append(pltpu.make_async_copy(done_q.at[:, cols], dq.at[:, cols], flush.at[p, 1]))
    cols = pl.ds(0, EARLY_KV)
    moves.append(pltpu.make_async_copy(done_k, dk.at[:, cols], flush.at[pieces, 0]))
    moves.append(pltpu.make_async_copy(done_v, dv.at[:, cols], flush.at[pieces, 1]))
    for move in moves:
        move.start()

    def one(n, first):
        return first + jnp.where(owners[n] < me, lens[n], 0)

    shift = lax.fori_loop(0, lens.shape[0], one, jnp.int32(0)) - (me * TOK - HALO)
    shift = jnp.clip(shift, 0, 2 * HALO)
    middle = slice(HALO, HALO + TOK)
    for ref, part in ((out_tall, out_part), (dq_tall, dq_part)):
        ref[:, middle, :] = part[:, middle, :]
    clear((out_tall, dq_tall))
    dk_tall[...] = dk_part[...]
    dv_tall[...] = dv_part[...]
    n = KV_HEADS - 1
    halo_pass(
        False, last_q, last_g, head_rows(kw, n), head_rows(vw, n), (None, None, bias_after), owned,
        out_tall, dq_tall, dk_tall, dv_tall, parcel,
    )
    shift_queries(shift, out_tall, dq_tall, stage_o, stage_q)
    shift_keys(shift, dk_tall, dv_tall, stage_k, stage_v)
    cols = pl.ds(EARLY_COLS, LAST_COLS)
    rest = [
        pltpu.make_async_copy(stage_o, out.at[:, cols], store.at[0]),
        pltpu.make_async_copy(stage_q, dq.at[:, cols], store.at[1]),
        pltpu.make_async_copy(stage_k, dk.at[:, kv_cols(n)], store.at[2]),
        pltpu.make_async_copy(stage_v, dv.at[:, kv_cols(n)], store.at[3]),
    ]
    for move in rest:
        move.start()
    for move in moves + rest:
        move.wait()


def local(devices, q, k, v, g, lens, owners, table):
    any_spec = pl.BlockSpec(memory_space=pl.ANY)
    vmem = pl.BlockSpec(memory_space=pltpu.VMEM)
    smem = pl.BlockSpec(memory_space=pltpu.SMEM)
    q, k, v, g, lens, owners, table = [
        pltpu.with_memory_space_constraint(x, pltpu.HBM) for x in (q, k, v, g, lens, owners, table)
    ]
    def tall(count):
        return pltpu.VMEM((count, TALL, HEAD_DIM), F32)

    def bias(b):
        return pltpu.VMEM((BLOCKS[b][3] - BLOCKS[b][2], CW), F32)

    def lent(u):
        return pltpu.VMEM((HALO, 2 * HALO * UNITS[u][2] + 2 * HEAD_DIM), BF16)

    kv_tall = pltpu.VMEM((TALL, HEAD_DIM), F32)
    units = len(UNITS)
    last_talls = [tall(UNITS[-1][2])] * 2 + [kv_tall] * 2
    mid_shapes = (
        [pltpu.VMEM((WIN, KV_COLS), BF16)] * 2
        + [bias(AFTER), pltpu.VMEM((len(BLOCKS), 8, CW), F32)]
        + [pltpu.VMEM((WIN, LAST_COLS), BF16)] * 2
        + [pltpu.VMEM((CAP, EARLY_COLS), BF16)] * 2
        + [pltpu.VMEM((CAP, EARLY_KV), BF16)] * 2
        + last_talls
        + [lent(units - 1)]
    )
    near = [pltpu.VMEM((WIN, count * HEAD_DIM), BF16) for _, _, count in UNITS[:-1] for _ in range(2)]
    talls = [tall(count) for _, _, count in UNITS[:-1] for _ in range(2)]
    dma = pltpu.SemaphoreType.DMA
    mid = pl.pallas_call(
        functools.partial(exchange_kernel, devices),
        out_shape=mid_shapes,
        in_specs=[any_spec] * 4 + [smem] * 3,
        out_specs=[vmem] * len(mid_shapes),
        scratch_shapes=[bias(0), bias(1), bias(LENT)]
        + near
        + talls
        + [kv_tall] * (2 * (KV_HEADS - 1))
        + [lent(u) for u in range(units - 1)]
        + [lent(u) for u in range(units)]
        + [pltpu.VMEM((HALO, GCOLS), BF16)] * 4
        + [dma((units, 2))] * 3
        + [dma((2, 2))] * 2
        + [dma((2,))]
        + [dma((units,))] * 2
        + [dma((3, 2))] * 2,
        compiler_params=pltpu.CompilerParams(
            collective_id=0, has_side_effects=True, vmem_limit_bytes=40 << 20
        ),
        name="exchange",
    )(q, g, k, v, lens, owners, table)
    mid = [pltpu.with_memory_space_constraint(x, pltpu.VMEM) for x in mid]
    shapes = [(CAP, w) for w in (HEADS * HEAD_DIM,) * 2 + (KV_COLS,) * 2]
    return tuple(
        pl.pallas_call(
            finish_kernel,
            out_shape=[pltpu.HBM(s, BF16) for s in shapes],
            in_specs=[smem] * 2 + [vmem] * len(mid),
            out_specs=[any_spec] * 4,
            scratch_shapes=[pltpu.VMEM((CAP, LAST_COLS), BF16)] * 2
            + [pltpu.VMEM((CAP, HEAD_DIM), BF16)] * 2
            + last_talls
            + [dma((5, 2)), dma((4,))],
            compiler_params=pltpu.CompilerParams(vmem_limit_bytes=24 << 20),
            name="finish",
        )(lens, owners, *mid)
    )


def solution(mesh):
    rows = P(("dp", "seq"), None)
    return jax.shard_map(
        functools.partial(local, mesh.shape["seq"]),
        mesh=mesh,
        in_specs=(rows, rows, rows, rows, P("dp"), P("dp"), P("dp", None)),
        out_specs=(rows, rows, rows, rows),
        check_vma=False,
    )
```

```python
import functools

import jax
import jax.numpy as jnp
from jax import lax
from jax.experimental import pallas as pl
from jax.experimental.pallas import tpu as pltpu
from jax.sharding import PartitionSpec as P

HEADS = 64
KV_HEADS = 8
HEAD_DIM = 128
BLOCK = 128
CAP = 192
HALO = 32
TOK = 128
WIN = TOK + 2 * HALO
GROUP = HEADS // KV_HEADS
GCOLS = GROUP * HEAD_DIM
QB = 64
CHUNK_HEADS = 4
CW = CHUNK_HEADS * QB
OWN_BLOCKS = ((HALO + QB, QB, 0, HALO + 2 * QB), (HALO, QB, 0, HALO + QB))
AFTER = 2
LENT = 3
BLOCKS = OWN_BLOCKS + ((HALO + TOK, HALO, 0, WIN), (TOK, HALO, TOK, HALO + TOK))
ROW = 4
TALL = CAP + 2 * HALO
INV_ROOT = HEAD_DIM**-0.5
LOG2E = 1.4426950408889634
FAR = -1e30
MESH = pl.DeviceIdType.MESH
BF16 = jnp.bfloat16
F32 = jnp.float32


def dot(a, b, dims):
    return lax.dot_general(a, b, (dims, ((), ())), preferred_element_type=F32)


def clear(tall_refs):
    for ref in tall_refs:
        tail = ref.shape[:-2] + (TALL - WIN, HEAD_DIM)
        ref[..., WIN:TALL, :] = jnp.zeros(tail, F32)


def prepare(me, devices, len_ref, own_ref, table_ref, biases, owned):
    docs = len_ref.shape[0]
    base = me * TOK - HALO
    key_pos = base + lax.broadcasted_iota(jnp.int32, (WIN, 128), 0)
    lane = lax.broadcasted_iota(jnp.int32, (8, CW), 1)
    query_pos = [base + first + lane % count for first, count, _, _ in BLOCKS]

    def one(n, carry):
        start, first, count, lent, key_doc, query_doc = carry
        length = len_ref[n]
        owner = own_ref[n]
        key_doc = key_doc + jnp.where(key_pos >= start, 1, 0)
        query_doc = tuple(
            d + jnp.where(p >= start, 1, 0) for d, p in zip(query_doc, query_pos)
        )
        first = first + jnp.where(owner < me, length, 0)
        count = count + jnp.where(owner == me, length, 0)
        lent = lent + jnp.where(owner == me + 1, length, 0)
        return (start + length, first, count, lent, key_doc, query_doc)

    zero = jnp.int32(0)
    _, first, count, lent, key_doc, query_doc = lax.fori_loop(
        0,
        docs,
        one,
        (
            zero,
            zero,
            zero,
            zero,
            jnp.zeros((WIN, 128), jnp.int32),
            tuple(jnp.zeros((8, CW), jnp.int32) for _ in BLOCKS),
        ),
    )
    before = jnp.maximum(me - 1, 0)
    after = jnp.minimum(me + 1, devices - 1)
    own_before = table_ref[me, before]
    after_own = table_ref[after, me]
    after_before = table_ref[after, before]
    key_pos2 = jnp.concatenate([key_pos] * (CW // 128), axis=1)
    key_doc2 = jnp.concatenate([key_doc] * (CW // 128), axis=1)
    for b, (_, _, low, high) in enumerate(BLOCKS):
        kp, kd = key_pos2[low:high], key_doc2[low:high]
        qp, qd = query_pos[b][:1], query_doc[b][:1]
        key_block = (kp + BLOCK) // BLOCK - me
        query_block = (qp + BLOCK) // BLOCK - me
        linked = jnp.where(
            query_block == 1,
            jnp.where(key_block == 0, own_before, 1),
            jnp.where(
                query_block == 2,
                jnp.where(key_block == 0, after_before, jnp.where(key_block == 1, after_own, 1)),
                1,
            ),
        )
        allowed = (kd == qd) & (kp <= qp) & (linked == 1)
        biases[b][...] = jnp.where(allowed, 0.0, FAR)
        begin, size = (first + count, lent) if b == LENT else (first, count)
        inside = (query_pos[b] >= begin) & (query_pos[b] < begin + size)
        owned[b] = jnp.where(inside, 1.0, 0.0)
    return jnp.clip(first - base, 0, 2 * HALO)


def head_rows(ref, n):
    cols = slice(n * HEAD_DIM, (n + 1) * HEAD_DIM)
    return lambda low, high: ref[low:high, cols]


def scores_of(job, q, g, k, v):
    b, heads = job
    first, count, low, high = BLOCKS[b]
    span = slice(first, first + count)
    qs = jnp.concatenate([q[span, h * HEAD_DIM : (h + 1) * HEAD_DIM] for h in heads], axis=0)
    gs = jnp.concatenate([g[span, h * HEAD_DIM : (h + 1) * HEAD_DIM] for h in heads], axis=0)
    return dot(k(low, high), qs, ((1,), (1,))), dot(v(low, high), gs, ((1,), (1,))), qs, gs


def softmax_of(job, scores, prob_grad, biases, owned):
    b, heads = job
    width = BLOCKS[b][1] * len(heads)
    scores = scores * (INV_ROOT * LOG2E) + biases[b][:, 0:width]
    highest = jnp.max(scores, axis=0, keepdims=True)
    raised = jnp.exp2(scores - highest)
    total = jnp.sum(raised, axis=0, keepdims=True)
    prob = raised * (owned[b, 0:1, 0:width] / total)
    delta = jnp.sum(prob * prob_grad, axis=0, keepdims=True)
    return prob.astype(BF16), (prob * (prob_grad - delta)).astype(BF16)


def query_rows(half, score_grad, first, count, heads, keys, values, out_tall, dq_tall):
    span = slice(first, first + count)
    out = dot(half, values, ((0,), (0,)))
    dq = dot(score_grad, keys, ((0,), (0,))) * INV_ROOT
    for i, h in enumerate(heads):
        out_tall[h, span, :] = out[i * count : (i + 1) * count]
        dq_tall[h, span, :] = dq[i * count : (i + 1) * count]


def key_terms(half, score_grad, qs, gs):
    return dot(score_grad, qs, ((1,), (0,))), dot(half, gs, ((1,), (0,)))


def run_jobs(jobs, fresh_rows, q, g, k, v, biases, owned, out_tall, dq_tall, dk_tall, dv_tall):
    first = [scores_of(job, q, g, k, v) for job in jobs]
    second = [softmax_of(job, f[0], f[1], biases, owned) for job, f in zip(jobs, first)]
    sums = {}
    for (b, heads), (_, _, qs, gs), (half, score_grad) in zip(jobs, first, second):
        start, count, low, high = BLOCKS[b]
        query_rows(half, score_grad, start, count, heads, k(low, high), v(low, high), out_tall, dq_tall)
        dk, dv = key_terms(half, score_grad, qs, gs)
        old = sums.get(b)
        sums[b] = (dk, dv) if old is None else (old[0] + dk, old[1] + dv)
    for b, (dk, dv) in sums.items():
        rows = BLOCKS[b][3]
        old = min(rows, fresh_rows)
        if old:
            dk_tall[0:old, :] += dk[0:old]
            dv_tall[0:old, :] += dv[0:old]
        if old < rows:
            dk_tall[old:rows, :] = dk[old:rows]
            dv_tall[old:rows, :] = dv[old:rows]
        fresh_rows = max(fresh_rows, rows)


def own_pass(fresh, q, *rest):
    count = q.shape[1] // HEAD_DIM
    jobs = [
        (b, range(c, min(c + CHUNK_HEADS, count)))
        for b in range(len(OWN_BLOCKS))
        for c in range(0, count, CHUNK_HEADS)
    ]
    run_jobs(jobs, 0 if fresh else WIN, q, *rest)


def lend_pass(q, g, k, v, biases, owned, parcel):
    job = (LENT, range(q.shape[1] // HEAD_DIM))
    scores, prob_grad, qs, gs = scores_of(job, q, g, k, v)
    half, score_grad = softmax_of(job, scores, prob_grad, biases, owned)
    width = half.shape[1]
    parcel[:, 0:width] = half
    parcel[:, width : 2 * width] = score_grad
    dk, dv = key_terms(half, score_grad, qs, gs)
    parcel[:, 2 * width : 2 * width + HEAD_DIM] = dk.astype(BF16)
    parcel[:, 2 * width + HEAD_DIM : 2 * width + 2 * HEAD_DIM] = dv.astype(BF16)


def halo_pass(fresh, q, g, k, v, biases, owned, out_tall, dq_tall, dk_tall, dv_tall, parcel):
    heads = range(q.shape[1] // HEAD_DIM)
    width = HALO * len(heads)
    query_rows(
        parcel[:, 0:width], parcel[:, width : 2 * width], 0, HALO, heads, k(0, HALO), v(0, HALO), out_tall, dq_tall
    )
    run_jobs(
        [(AFTER, heads)], HALO + TOK if fresh else WIN, q, g, k, v, biases, owned, out_tall, dq_tall, dk_tall, dv_tall
    )
    dk_tall[0:HALO, :] += parcel[:, 2 * width : 2 * width + HEAD_DIM].astype(F32)
    dv_tall[0:HALO, :] += parcel[:, 2 * width + HEAD_DIM : 2 * width + 2 * HEAD_DIM].astype(F32)


def shift_queries(shift, out_tall, dq_tall, out, dq):
    rows = pl.ds(shift, CAP)
    for h in range(out.shape[1] // HEAD_DIM):
        cols = slice(h * HEAD_DIM, (h + 1) * HEAD_DIM)
        out[:, cols] = out_tall[h, rows, :].astype(BF16)
        dq[:, cols] = dq_tall[h, rows, :].astype(BF16)


def shift_keys(shift, dk_tall, dv_tall, dk, dv):
    rows = pl.ds(shift, CAP)
    dk[...] = (dk_tall[rows, :] * INV_ROOT).astype(BF16)
    dv[...] = dv_tall[rows, :].astype(BF16)


AHEAD = 7
LEND_CUTS = (4, 6)
RELAY_AT = (3, 6)
RELAYED = (6, 7)
LAST_HEADS = 4
UNITS = [(n, 0, GROUP) for n in range(KV_HEADS - 1)] + [
    (KV_HEADS - 1, 0, GROUP - LAST_HEADS),
    (KV_HEADS - 1, GROUP - LAST_HEADS, LAST_HEADS),
]
LAST_COLS = UNITS[-1][2] * HEAD_DIM
EARLY_COLS = HEADS * HEAD_DIM - LAST_COLS
KV_COLS = KV_HEADS * HEAD_DIM
EARLY_KV = KV_COLS - HEAD_DIM


def unit_cols(u):
    n, first, count = UNITS[u]
    return pl.ds(n * GCOLS + first * HEAD_DIM, count * HEAD_DIM)


def kv_cols(n):
    return pl.ds(n * HEAD_DIM, HEAD_DIM)


def exchange_kernel(devices, *refs):
    refs = list(refs)

    def take(count):
        taken = refs[:count]
        del refs[:count]
        return taken

    def pairs(count):
        return [take(2) for _ in range(count)]

    units = len(UNITS)
    early = units - 1
    q, g, k, v, lens, owners, table = take(7)
    kw, vw, bias_after, owned, last_q, last_g, done_o, done_q, done_k, done_v = take(10)
    last_talls, last_kv_talls = pairs(2)
    last_lent = take(1)
    biases = take(2) + [bias_after] + take(1)
    near = pairs(early) + [(last_q, last_g)]
    talls = pairs(early) + [last_talls]
    kv_talls = pairs(KV_HEADS - 1) + [last_kv_talls]
    lent = take(early) + last_lent
    lend = take(units)
    relay = [pairs(len(RELAYED)) for _ in range(2)]
    send, recv, load, kv_send, kv_recv, kv_load, lend_send, lend_recv, relay_send, relay_recv = take(10)
    dp = lax.axis_index("dp")
    me = lax.axis_index("seq")
    x = lax.rem(me, ROW)
    has = (me < devices - 1, me > 0)
    peer = (jnp.minimum(me + 1, devices - 1), jnp.maximum(me - 1, 0))
    near_row = me - x + lax.rem(x + 1, ROW)
    above = (x == 0) | ((x == 1) & (me < devices - ROW))
    below = (x == ROW - 1) | ((x == 0) & (me > 0))
    relay_to = jnp.maximum(jnp.where(x == 0, me - 3, near_row), 0)
    relayed = (me != 0, me != devices - 3, me != devices - 2, me != devices - 1)
    relay_when = (relayed, tuple(ok & (x == step) for step, ok in enumerate(relayed)))

    def remote(src, dst, target, send_sem, recv_sem):
        return pltpu.make_async_remote_copy(
            src_ref=src, dst_ref=dst, send_sem=send_sem, recv_sem=recv_sem, device_id=(dp, target), device_id_type=MESH
        )

    def hop(src, cols, dst, side, sems):
        rows = pl.ds(TOK - HALO, HALO) if side == 0 else pl.ds(0, HALO)
        there = pl.ds(0, HALO) if side == 0 else pl.ds(HALO + TOK, HALO)
        return remote(src.at[rows, cols], dst.at[there, :], peer[side], *sems)

    def own(src, cols, dst, sem):
        return pltpu.make_async_copy(src.at[:, cols], dst.at[pl.ds(HALO, TOK), :], sem)

    every = pl.ds(0, KV_COLS)
    kv = ((k, kw), (v, vw))
    kv_hops = [
        [hop(src, every, dst, side, (kv_send.at[a, side], kv_recv.at[a, side])) for a, (src, dst) in enumerate(kv)]
        for side in range(2)
    ]
    kv_own = [own(src, every, dst, kv_load.at[a]) for a, (src, dst) in enumerate(kv)]
    hops = [
        [
            hop(src, unit_cols(u), near[u][a], 1, (send.at[u, a], recv.at[u, a]))
            for a, src in enumerate((q, g))
            if u != RELAYED[0]
        ]
        for u in range(units)
    ]
    lends = [
        [remote(lend[u], lent[u], peer[0], lend_send.at[u], lend_recv.at[u])] for u in range(units)
    ]
    after = pl.ds(HALO + TOK, HALO)
    relays = [[[] for _ in RELAYED] for _ in range(3)]
    for i, u in enumerate(RELAYED):
        for a, src in enumerate((q, g)):
            first, second = relay[0][i][a], relay[1][i][a]
            path = (
                (src.at[pl.ds(0, HALO), unit_cols(u)], first, relay_to),
                (first, second, near_row),
                (second, near[u][a].at[after, :], near_row),
            )
            for step, (here, there, target) in enumerate(path):
                relays[step][i].append(
                    remote(here, there, target, relay_send.at[step, i, a], relay_recv.at[step, i, a])
                )
    owns = [
        [own(src, unit_cols(u), near[u][a], load.at[u, a]) for a, src in enumerate((q, g))]
        for u in range(units)
    ]

    barrier = pltpu.get_barrier_semaphore()
    greet = ((has[0], peer[0]), (has[1], peer[1]), (above, jnp.minimum(me + 3, devices - 1)), (below, jnp.maximum(me - 3, 0)))
    peers = jnp.int32(0)
    for meets, other in greet:
        peers = peers + jnp.where(meets, 1, 0)

        @pl.when(meets)
        def _():
            pl.semaphore_signal(barrier, inc=1, device_id=(dp, other), device_id_type=MESH)

    def start(copies):
        for copy in copies:
            copy.start()

    pl.semaphore_wait(barrier, peers)

    def arrive(copies, sends, receives):
        @pl.when(sends)
        def _():
            for copy in copies:
                copy.wait_send()

        @pl.when(receives)
        def _():
            for copy in copies:
                copy.wait_recv()

    for side in (0, 1):

        @pl.when(has[side])
        def _():
            start(kv_hops[side])

    def relay_start(step):
        for copies, ok in zip(relays[step], relay_when):

            @pl.when(ok[step])
            def _():
                start(copies)

    def relay_arrive(step, i):
        arrive(relays[step][i], relay_when[i][step], relay_when[i][step + 1])

    direct = [has for _ in range(units)]
    direct[RELAYED[1]] = (has[0] & (x != ROW - 1), has[1] & (x != 0))
    relay_start(0)
    for u in range(units):
        if u != RELAYED[0]:

            @pl.when(direct[u][1])
            def _():
                start(hops[u])

    start(kv_own)
    for copies in owns:
        start(copies)

    def fill(ref, rows):
        ref[rows, :] = jnp.zeros((HALO, ref.shape[1]), ref.dtype)

    @pl.when(me == 0)
    def _():
        for ref in lent + [kw, vw]:
            fill(ref, pl.ds(0, HALO))

    @pl.when(me == devices - 1)
    def _():
        for ref in [r for pair in near for r in pair] + [kw, vw]:
            fill(ref, after)

    shift = prepare(me, devices, lens, owners, table, biases, owned)
    for pair in talls + kv_talls:
        clear(pair)

    def columns(u):
        return head_rows(kw, UNITS[u][0]), head_rows(vw, UNITS[u][0])

    def operands(u):
        n, first, _ = UNITS[u]
        return (first == 0, *near[u], *columns(u), biases, owned, *talls[u], *kv_talls[n])

    def lend_rows(u):
        for copy in owns[u]:
            copy.wait()
        lend_pass(*near[u], *columns(u), biases, owned, lend[u])

    def lend_out(first, last):
        @pl.when(has[0])
        def _():
            for copies in lends[first:last]:
                start(copies)

    for copy in kv_own:
        copy.wait()
    for u in range(units):
        lend_rows(u)
    lend_out(0, LEND_CUTS[0])
    arrive(kv_hops[0], has[0], has[1])
    for u in range(RELAY_AT[0]):
        own_pass(*operands(u))
    for i in range(len(RELAYED)):
        relay_arrive(0, i)
    relay_start(1)
    lend_out(*LEND_CUTS[0:2])
    for u in range(*RELAY_AT):
        own_pass(*operands(u))
    for i in range(len(RELAYED)):
        relay_arrive(1, i)
    relay_start(2)
    lend_out(LEND_CUTS[1], units)
    for u in range(RELAY_AT[1], AHEAD):
        own_pass(*operands(u))
    arrive(kv_hops[1], has[1], has[0])
    for u, (n, first, count) in enumerate(UNITS):
        if u + AHEAD < units:
            own_pass(*operands(u + AHEAD))
        if u in RELAYED:
            relay_arrive(2, RELAYED.index(u))
        if u != RELAYED[0]:
            arrive(hops[u], direct[u][1], direct[u][0])
        arrive(lends[u], has[0], has[1])
        if u == early:
            break
        halo_pass(*operands(u), lent[u])
        shift_queries(shift, *talls[u], done_o.at[:, unit_cols(u)], done_q.at[:, unit_cols(u)])
        if first + count == GROUP:
            shift_keys(shift, *kv_talls[n], done_k.at[:, kv_cols(n)], done_v.at[:, kv_cols(n)])


def finish_kernel(lens, owners, kw, vw, bias_after, owned, last_q, last_g, done_o, done_q, done_k, done_v,
                  out_part, dq_part, dk_part, dv_part, parcel, out, dq, dk, dv, stage_o, stage_q, stage_k, stage_v,
                  out_tall, dq_tall, dk_tall, dv_tall, flush, store):
    me = lax.axis_index("seq")
    pieces = 2
    width = EARLY_COLS // pieces
    moves = []
    for p in range(pieces):
        cols = pl.ds(p * width, width)
        moves.append(pltpu.make_async_copy(done_o.at[:, cols], out.at[:, cols], flush.at[p, 0]))
        moves.append(pltpu.make_async_copy(done_q.at[:, cols], dq.at[:, cols], flush.at[p, 1]))
    cols = pl.ds(0, EARLY_KV)
    moves.append(pltpu.make_async_copy(done_k, dk.at[:, cols], flush.at[pieces, 0]))
    moves.append(pltpu.make_async_copy(done_v, dv.at[:, cols], flush.at[pieces, 1]))
    for move in moves:
        move.start()

    def one(n, first):
        return first + jnp.where(owners[n] < me, lens[n], 0)

    shift = lax.fori_loop(0, lens.shape[0], one, jnp.int32(0)) - (me * TOK - HALO)
    shift = jnp.clip(shift, 0, 2 * HALO)
    middle = slice(HALO, HALO + TOK)
    for ref, part in ((out_tall, out_part), (dq_tall, dq_part)):
        ref[:, middle, :] = part[:, middle, :]
    clear((out_tall, dq_tall))
    dk_tall[...] = dk_part[...]
    dv_tall[...] = dv_part[...]
    n = KV_HEADS - 1
    halo_pass(
        False, last_q, last_g, head_rows(kw, n), head_rows(vw, n), (None, None, bias_after), owned,
        out_tall, dq_tall, dk_tall, dv_tall, parcel,
    )
    shift_queries(shift, out_tall, dq_tall, stage_o, stage_q)
    shift_keys(shift, dk_tall, dv_tall, stage_k, stage_v)
    cols = pl.ds(EARLY_COLS, LAST_COLS)
    rest = [
        pltpu.make_async_copy(stage_o, out.at[:, cols], store.at[0]),
        pltpu.make_async_copy(stage_q, dq.at[:, cols], store.at[1]),
        pltpu.make_async_copy(stage_k, dk.at[:, kv_cols(n)], store.at[2]),
        pltpu.make_async_copy(stage_v, dv.at[:, kv_cols(n)], store.at[3]),
    ]
    for move in rest:
        move.start()
    for move in moves + rest:
        move.wait()


def local(devices, q, k, v, g, lens, owners, table):
    any_spec = pl.BlockSpec(memory_space=pl.ANY)
    vmem = pl.BlockSpec(memory_space=pltpu.VMEM)
    smem = pl.BlockSpec(memory_space=pltpu.SMEM)
    q, k, v, g, lens, owners, table = [
        pltpu.with_memory_space_constraint(x, pltpu.HBM) for x in (q, k, v, g, lens, owners, table)
    ]
    def tall(count):
        return pltpu.VMEM((count, TALL, HEAD_DIM), F32)

    def bias(b):
        return pltpu.VMEM((BLOCKS[b][3] - BLOCKS[b][2], CW), F32)

    def lent(u):
        return pltpu.VMEM((HALO, 2 * HALO * UNITS[u][2] + 2 * HEAD_DIM), BF16)

    kv_tall = pltpu.VMEM((TALL, HEAD_DIM), F32)
    units = len(UNITS)
    last_talls = [tall(UNITS[-1][2])] * 2 + [kv_tall] * 2
    mid_shapes = (
        [pltpu.VMEM((WIN, KV_COLS), BF16)] * 2
        + [bias(AFTER), pltpu.VMEM((len(BLOCKS), 8, CW), F32)]
        + [pltpu.VMEM((WIN, LAST_COLS), BF16)] * 2
        + [pltpu.VMEM((CAP, EARLY_COLS), BF16)] * 2
        + [pltpu.VMEM((CAP, EARLY_KV), BF16)] * 2
        + last_talls
        + [lent(units - 1)]
    )
    near = [pltpu.VMEM((WIN, count * HEAD_DIM), BF16) for _, _, count in UNITS[:-1] for _ in range(2)]
    talls = [tall(count) for _, _, count in UNITS[:-1] for _ in range(2)]
    dma = pltpu.SemaphoreType.DMA
    mid = pl.pallas_call(
        functools.partial(exchange_kernel, devices),
        out_shape=mid_shapes,
        in_specs=[any_spec] * 4 + [smem] * 3,
        out_specs=[vmem] * len(mid_shapes),
        scratch_shapes=[bias(0), bias(1), bias(LENT)]
        + near
        + talls
        + [kv_tall] * (2 * (KV_HEADS - 1))
        + [lent(u) for u in range(units - 1)]
        + [lent(u) for u in range(units)]
        + [pltpu.VMEM((HALO, UNITS[u][2] * HEAD_DIM), BF16) for _ in range(2) for u in RELAYED for _ in range(2)]
        + [dma((units, 2))] * 3
        + [dma((2, 2))] * 2
        + [dma((2,))]
        + [dma((units,))] * 2
        + [dma((3, len(RELAYED), 2))] * 2,
        compiler_params=pltpu.CompilerParams(
            collective_id=0, has_side_effects=True, vmem_limit_bytes=40 << 20
        ),
        name="exchange",
    )(q, g, k, v, lens, owners, table)
    mid = [pltpu.with_memory_space_constraint(x, pltpu.VMEM) for x in mid]
    shapes = [(CAP, w) for w in (HEADS * HEAD_DIM,) * 2 + (KV_COLS,) * 2]
    return tuple(
        pl.pallas_call(
            finish_kernel,
            out_shape=[pltpu.HBM(s, BF16) for s in shapes],
            in_specs=[smem] * 2 + [vmem] * len(mid),
            out_specs=[any_spec] * 4,
            scratch_shapes=[pltpu.VMEM((CAP, LAST_COLS), BF16)] * 2
            + [pltpu.VMEM((CAP, HEAD_DIM), BF16)] * 2
            + last_talls
            + [dma((3, 2)), dma((4,))],
            compiler_params=pltpu.CompilerParams(vmem_limit_bytes=24 << 20),
            name="finish",
        )(lens, owners, *mid)
    )


def solution(mesh):
    rows = P(("dp", "seq"), None)
    return jax.shard_map(
        functools.partial(local, mesh.shape["seq"]),
        mesh=mesh,
        in_specs=(rows, rows, rows, rows, P("dp"), P("dp"), P("dp", None)),
        out_specs=(rows, rows, rows, rows),
        check_vma=False,
    )
```

```python
import functools

import jax
import jax.numpy as jnp
from jax import lax
from jax.experimental import pallas as pl
from jax.experimental.pallas import tpu as pltpu
from jax.sharding import PartitionSpec as P

HEADS = 64
KV_HEADS = 8
HEAD_DIM = 128
BLOCK = 128
CAP = 192
HALO = 32
TOK = 128
WIN = TOK + 2 * HALO
GROUP = HEADS // KV_HEADS
GCOLS = GROUP * HEAD_DIM
QB = 64
CHUNK_HEADS = 4
CW = CHUNK_HEADS * QB
OWN_BLOCKS = ((HALO + QB, QB, 0, HALO + 2 * QB), (HALO, QB, 0, HALO + QB))
AFTER = 2
LENT = 3
BLOCKS = OWN_BLOCKS + ((HALO + TOK, HALO, 0, WIN), (TOK, HALO, TOK, HALO + TOK))
ROW = 4
TALL = CAP + 2 * HALO
INV_ROOT = HEAD_DIM**-0.5
LOG2E = 1.4426950408889634
FAR = -1e30
MESH = pl.DeviceIdType.MESH
BF16 = jnp.bfloat16
F32 = jnp.float32


def dot(a, b, dims):
    return lax.dot_general(a, b, (dims, ((), ())), preferred_element_type=F32)


def clear(tall_refs):
    for ref in tall_refs:
        tail = ref.shape[:-2] + (TALL - WIN, HEAD_DIM)
        ref[..., WIN:TALL, :] = jnp.zeros(tail, F32)


def prepare(me, devices, len_ref, own_ref, table_ref, biases, owned):
    docs = len_ref.shape[0]
    base = me * TOK - HALO
    key_pos = base + lax.broadcasted_iota(jnp.int32, (WIN, 128), 0)
    lane = lax.broadcasted_iota(jnp.int32, (8, CW), 1)
    query_pos = [base + first + lane % count for first, count, _, _ in BLOCKS]

    def one(n, carry):
        start, first, count, lent, key_doc, query_doc = carry
        length = len_ref[n]
        owner = own_ref[n]
        key_doc = key_doc + jnp.where(key_pos >= start, 1, 0)
        query_doc = tuple(
            d + jnp.where(p >= start, 1, 0) for d, p in zip(query_doc, query_pos)
        )
        first = first + jnp.where(owner < me, length, 0)
        count = count + jnp.where(owner == me, length, 0)
        lent = lent + jnp.where(owner == me + 1, length, 0)
        return (start + length, first, count, lent, key_doc, query_doc)

    zero = jnp.int32(0)
    _, first, count, lent, key_doc, query_doc = lax.fori_loop(
        0,
        docs,
        one,
        (
            zero,
            zero,
            zero,
            zero,
            jnp.zeros((WIN, 128), jnp.int32),
            tuple(jnp.zeros((8, CW), jnp.int32) for _ in BLOCKS),
        ),
    )
    before = jnp.maximum(me - 1, 0)
    after = jnp.minimum(me + 1, devices - 1)
    own_before = table_ref[me, before]
    after_own = table_ref[after, me]
    after_before = table_ref[after, before]
    key_pos2 = jnp.concatenate([key_pos] * (CW // 128), axis=1)
    key_doc2 = jnp.concatenate([key_doc] * (CW // 128), axis=1)
    for b, (_, _, low, high) in enumerate(BLOCKS):
        kp, kd = key_pos2[low:high], key_doc2[low:high]
        qp, qd = query_pos[b][:1], query_doc[b][:1]
        key_block = (kp + BLOCK) // BLOCK - me
        query_block = (qp + BLOCK) // BLOCK - me
        linked = jnp.where(
            query_block == 1,
            jnp.where(key_block == 0, own_before, 1),
            jnp.where(
                query_block == 2,
                jnp.where(key_block == 0, after_before, jnp.where(key_block == 1, after_own, 1)),
                1,
            ),
        )
        allowed = (kd == qd) & (kp <= qp) & (linked == 1)
        biases[b][...] = jnp.where(allowed, 0.0, FAR)
        begin, size = (first + count, lent) if b == LENT else (first, count)
        inside = (query_pos[b] >= begin) & (query_pos[b] < begin + size)
        owned[b] = jnp.where(inside, 1.0, 0.0)
    return jnp.clip(first - base, 0, 2 * HALO)


def head_rows(ref, n):
    cols = slice(n * HEAD_DIM, (n + 1) * HEAD_DIM)
    return lambda low, high: ref[low:high, cols]


def scores_of(job, q, g, k, v):
    b, heads = job
    first, count, low, high = BLOCKS[b]
    span = slice(first, first + count)
    qs = jnp.concatenate([q[span, h * HEAD_DIM : (h + 1) * HEAD_DIM] for h in heads], axis=0)
    gs = jnp.concatenate([g[span, h * HEAD_DIM : (h + 1) * HEAD_DIM] for h in heads], axis=0)
    return dot(k(low, high), qs, ((1,), (1,))), dot(v(low, high), gs, ((1,), (1,))), qs, gs


def softmax_of(job, scores, prob_grad, biases, owned):
    b, heads = job
    width = BLOCKS[b][1] * len(heads)
    scores = scores * (INV_ROOT * LOG2E) + biases[b][:, 0:width]
    highest = jnp.max(scores, axis=0, keepdims=True)
    raised = jnp.exp2(scores - highest)
    total = jnp.sum(raised, axis=0, keepdims=True)
    prob = raised * (owned[b, 0:1, 0:width] / total)
    delta = jnp.sum(prob * prob_grad, axis=0, keepdims=True)
    return prob.astype(BF16), (prob * (prob_grad - delta)).astype(BF16)


def query_rows(half, score_grad, first, count, heads, keys, values, out_tall, dq_tall):
    span = slice(first, first + count)
    out = dot(half, values, ((0,), (0,)))
    dq = dot(score_grad, keys, ((0,), (0,))) * INV_ROOT
    for i, h in enumerate(heads):
        out_tall[h, span, :] = out[i * count : (i + 1) * count]
        dq_tall[h, span, :] = dq[i * count : (i + 1) * count]


def key_terms(half, score_grad, qs, gs):
    return dot(score_grad, qs, ((1,), (0,))), dot(half, gs, ((1,), (0,)))


def run_jobs(jobs, fresh_rows, q, g, k, v, biases, owned, out_tall, dq_tall, dk_tall, dv_tall):
    first = [scores_of(job, q, g, k, v) for job in jobs]
    second = [softmax_of(job, f[0], f[1], biases, owned) for job, f in zip(jobs, first)]
    sums = {}
    for (b, heads), (_, _, qs, gs), (half, score_grad) in zip(jobs, first, second):
        start, count, low, high = BLOCKS[b]
        query_rows(half, score_grad, start, count, heads, k(low, high), v(low, high), out_tall, dq_tall)
        dk, dv = key_terms(half, score_grad, qs, gs)
        old = sums.get(b)
        sums[b] = (dk, dv) if old is None else (old[0] + dk, old[1] + dv)
    for b, (dk, dv) in sums.items():
        rows = BLOCKS[b][3]
        old = min(rows, fresh_rows)
        if old:
            dk_tall[0:old, :] += dk[0:old]
            dv_tall[0:old, :] += dv[0:old]
        if old < rows:
            dk_tall[old:rows, :] = dk[old:rows]
            dv_tall[old:rows, :] = dv[old:rows]
        fresh_rows = max(fresh_rows, rows)


def own_pass(fresh, q, *rest):
    count = q.shape[1] // HEAD_DIM
    jobs = [
        (b, range(c, min(c + CHUNK_HEADS, count)))
        for b in range(len(OWN_BLOCKS))
        for c in range(0, count, CHUNK_HEADS)
    ]
    run_jobs(jobs, 0 if fresh else WIN, q, *rest)


def lend_pass(q, g, k, v, biases, owned, parcel):
    job = (LENT, range(q.shape[1] // HEAD_DIM))
    scores, prob_grad, qs, gs = scores_of(job, q, g, k, v)
    half, score_grad = softmax_of(job, scores, prob_grad, biases, owned)
    width = half.shape[1]
    parcel[:, 0:width] = half
    parcel[:, width : 2 * width] = score_grad
    dk, dv = key_terms(half, score_grad, qs, gs)
    parcel[:, 2 * width : 2 * width + HEAD_DIM] = dk.astype(BF16)
    parcel[:, 2 * width + HEAD_DIM : 2 * width + 2 * HEAD_DIM] = dv.astype(BF16)


def halo_pass(fresh, q, g, k, v, biases, owned, out_tall, dq_tall, dk_tall, dv_tall, parcel):
    heads = range(q.shape[1] // HEAD_DIM)
    width = HALO * len(heads)
    query_rows(
        parcel[:, 0:width], parcel[:, width : 2 * width], 0, HALO, heads, k(0, HALO), v(0, HALO), out_tall, dq_tall
    )
    run_jobs(
        [(AFTER, heads)], HALO + TOK if fresh else WIN, q, g, k, v, biases, owned, out_tall, dq_tall, dk_tall, dv_tall
    )
    dk_tall[0:HALO, :] += parcel[:, 2 * width : 2 * width + HEAD_DIM].astype(F32)
    dv_tall[0:HALO, :] += parcel[:, 2 * width + HEAD_DIM : 2 * width + 2 * HEAD_DIM].astype(F32)


def shift_queries(shift, out_tall, dq_tall, out, dq):
    rows = pl.ds(shift, CAP)
    for h in range(out.shape[1] // HEAD_DIM):
        cols = slice(h * HEAD_DIM, (h + 1) * HEAD_DIM)
        out[:, cols] = out_tall[h, rows, :].astype(BF16)
        dq[:, cols] = dq_tall[h, rows, :].astype(BF16)


def shift_keys(shift, dk_tall, dv_tall, dk, dv):
    rows = pl.ds(shift, CAP)
    dk[...] = (dk_tall[rows, :] * INV_ROOT).astype(BF16)
    dv[...] = dv_tall[rows, :].astype(BF16)


AHEAD = 7
LEND_CUTS = (4, 6)
RELAY_AT = (3, 6)
RELAYED = (6, 7)
LAST_HEADS = 2
UNITS = [(n, 0, GROUP) for n in range(KV_HEADS - 1)] + [
    (KV_HEADS - 1, 0, GROUP - LAST_HEADS),
    (KV_HEADS - 1, GROUP - LAST_HEADS, LAST_HEADS),
]
LAST_COLS = UNITS[-1][2] * HEAD_DIM
EARLY_COLS = HEADS * HEAD_DIM - LAST_COLS
KV_COLS = KV_HEADS * HEAD_DIM
EARLY_KV = KV_COLS - HEAD_DIM


def unit_cols(u):
    n, first, count = UNITS[u]
    return pl.ds(n * GCOLS + first * HEAD_DIM, count * HEAD_DIM)


def kv_cols(n):
    return pl.ds(n * HEAD_DIM, HEAD_DIM)


def exchange_kernel(devices, *refs):
    refs = list(refs)

    def take(count):
        taken = refs[:count]
        del refs[:count]
        return taken

    def pairs(count):
        return [take(2) for _ in range(count)]

    units = len(UNITS)
    early = units - 1
    q, g, k, v, lens, owners, table = take(7)
    kw, vw, bias_after, owned, last_q, last_g, done_o, done_q, done_k, done_v = take(10)
    last_talls, last_kv_talls = pairs(2)
    last_lent = take(1)
    biases = take(2) + [bias_after] + take(1)
    near = pairs(early) + [(last_q, last_g)]
    talls = pairs(early) + [last_talls]
    kv_talls = pairs(KV_HEADS - 1) + [last_kv_talls]
    lent = take(early) + last_lent
    lend = take(units)
    relay = [pairs(len(RELAYED)) for _ in range(2)]
    send, recv, load, kv_send, kv_recv, kv_load, lend_send, lend_recv, relay_send, relay_recv = take(10)
    dp = lax.axis_index("dp")
    me = lax.axis_index("seq")
    x = lax.rem(me, ROW)
    has = (me < devices - 1, me > 0)
    peer = (jnp.minimum(me + 1, devices - 1), jnp.maximum(me - 1, 0))
    near_row = me - x + lax.rem(x + 1, ROW)
    above = (x == 0) | ((x == 1) & (me < devices - ROW))
    below = (x == ROW - 1) | ((x == 0) & (me > 0))
    relay_to = jnp.maximum(jnp.where(x == 0, me - 3, near_row), 0)
    relayed = (me != 0, me != devices - 3, me != devices - 2, me != devices - 1)
    relay_when = (relayed, tuple(ok & (x == step) for step, ok in enumerate(relayed)))

    def remote(src, dst, target, send_sem, recv_sem):
        return pltpu.make_async_remote_copy(
            src_ref=src, dst_ref=dst, send_sem=send_sem, recv_sem=recv_sem, device_id=(dp, target), device_id_type=MESH
        )

    def hop(src, cols, dst, side, sems):
        rows = pl.ds(TOK - HALO, HALO) if side == 0 else pl.ds(0, HALO)
        there = pl.ds(0, HALO) if side == 0 else pl.ds(HALO + TOK, HALO)
        return remote(src.at[rows, cols], dst.at[there, :], peer[side], *sems)

    def own(src, cols, dst, sem):
        return pltpu.make_async_copy(src.at[:, cols], dst.at[pl.ds(HALO, TOK), :], sem)

    every = pl.ds(0, KV_COLS)
    kv = ((k, kw), (v, vw))
    kv_hops = [
        [hop(src, every, dst, side, (kv_send.at[a, side], kv_recv.at[a, side])) for a, (src, dst) in enumerate(kv)]
        for side in range(2)
    ]
    kv_own = [own(src, every, dst, kv_load.at[a]) for a, (src, dst) in enumerate(kv)]
    hops = [
        [
            hop(src, unit_cols(u), near[u][a], 1, (send.at[u, a], recv.at[u, a]))
            for a, src in enumerate((q, g))
            if u != RELAYED[0]
        ]
        for u in range(units)
    ]
    lends = [
        [remote(lend[u], lent[u], peer[0], lend_send.at[u], lend_recv.at[u])] for u in range(units)
    ]
    after = pl.ds(HALO + TOK, HALO)
    relays = [[[] for _ in RELAYED] for _ in range(3)]
    for i, u in enumerate(RELAYED):
        for a, src in enumerate((q, g)):
            first, second = relay[0][i][a], relay[1][i][a]
            path = (
                (src.at[pl.ds(0, HALO), unit_cols(u)], first, relay_to),
                (first, second, near_row),
                (second, near[u][a].at[after, :], near_row),
            )
            for step, (here, there, target) in enumerate(path):
                relays[step][i].append(
                    remote(here, there, target, relay_send.at[step, i, a], relay_recv.at[step, i, a])
                )
    owns = [
        [own(src, unit_cols(u), near[u][a], load.at[u, a]) for a, src in enumerate((q, g))]
        for u in range(units)
    ]

    barrier = pltpu.get_barrier_semaphore()
    greet = ((has[0], peer[0]), (has[1], peer[1]), (above, jnp.minimum(me + 3, devices - 1)), (below, jnp.maximum(me - 3, 0)))
    peers = jnp.int32(0)
    for meets, other in greet:
        peers = peers + jnp.where(meets, 1, 0)

        @pl.when(meets)
        def _():
            pl.semaphore_signal(barrier, inc=1, device_id=(dp, other), device_id_type=MESH)

    def start(copies):
        for copy in copies:
            copy.start()

    pl.semaphore_wait(barrier, peers)

    def arrive(copies, sends, receives):
        @pl.when(sends)
        def _():
            for copy in copies:
                copy.wait_send()

        @pl.when(receives)
        def _():
            for copy in copies:
                copy.wait_recv()

    for side in (0, 1):

        @pl.when(has[side])
        def _():
            start(kv_hops[side])

    def relay_start(step):
        for copies, ok in zip(relays[step], relay_when):

            @pl.when(ok[step])
            def _():
                start(copies)

    def relay_arrive(step, i):
        arrive(relays[step][i], relay_when[i][step], relay_when[i][step + 1])

    direct = [has for _ in range(units)]
    direct[RELAYED[1]] = (has[0] & (x != ROW - 1), has[1] & (x != 0))
    relay_start(0)
    for u in range(units):
        if u != RELAYED[0]:

            @pl.when(direct[u][1])
            def _():
                start(hops[u])

    start(kv_own)
    for copies in owns:
        start(copies)

    def fill(ref, rows):
        ref[rows, :] = jnp.zeros((HALO, ref.shape[1]), ref.dtype)

    @pl.when(me == 0)
    def _():
        for ref in lent + [kw, vw]:
            fill(ref, pl.ds(0, HALO))

    @pl.when(me == devices - 1)
    def _():
        for ref in [r for pair in near for r in pair] + [kw, vw]:
            fill(ref, after)

    shift = prepare(me, devices, lens, owners, table, biases, owned)
    for pair in talls + kv_talls:
        clear(pair)

    def columns(u):
        return head_rows(kw, UNITS[u][0]), head_rows(vw, UNITS[u][0])

    def operands(u):
        n, first, _ = UNITS[u]
        return (first == 0, *near[u], *columns(u), biases, owned, *talls[u], *kv_talls[n])

    def lend_rows(u):
        for copy in owns[u]:
            copy.wait()
        lend_pass(*near[u], *columns(u), biases, owned, lend[u])

    def lend_out(first, last):
        @pl.when(has[0])
        def _():
            for copies in lends[first:last]:
                start(copies)

    for copy in kv_own:
        copy.wait()
    for u in range(units):
        lend_rows(u)
    lend_out(0, LEND_CUTS[0])
    arrive(kv_hops[0], has[0], has[1])
    for u in range(RELAY_AT[0]):
        own_pass(*operands(u))
    for i in range(len(RELAYED)):
        relay_arrive(0, i)
    relay_start(1)
    lend_out(*LEND_CUTS[0:2])
    for u in range(*RELAY_AT):
        own_pass(*operands(u))
    for i in range(len(RELAYED)):
        relay_arrive(1, i)
    relay_start(2)
    lend_out(LEND_CUTS[1], units)
    for u in range(RELAY_AT[1], AHEAD):
        own_pass(*operands(u))
    arrive(kv_hops[1], has[1], has[0])
    for u, (n, first, count) in enumerate(UNITS):
        if u + AHEAD < units:
            own_pass(*operands(u + AHEAD))
        if u in RELAYED:
            relay_arrive(2, RELAYED.index(u))
        if u != RELAYED[0]:
            arrive(hops[u], direct[u][1], direct[u][0])
        arrive(lends[u], has[0], has[1])
        if u == early:
            break
        halo_pass(*operands(u), lent[u])
        shift_queries(shift, *talls[u], done_o.at[:, unit_cols(u)], done_q.at[:, unit_cols(u)])
        if first + count == GROUP:
            shift_keys(shift, *kv_talls[n], done_k.at[:, kv_cols(n)], done_v.at[:, kv_cols(n)])


def finish_kernel(lens, owners, kw, vw, bias_after, owned, last_q, last_g, done_o, done_q, done_k, done_v,
                  out_part, dq_part, dk_part, dv_part, parcel, out, dq, dk, dv, stage_o, stage_q, stage_k, stage_v,
                  out_tall, dq_tall, dk_tall, dv_tall, flush, store):
    me = lax.axis_index("seq")
    pieces = 2
    width = EARLY_COLS // pieces
    moves = []
    for p in range(pieces):
        cols = pl.ds(p * width, width)
        moves.append(pltpu.make_async_copy(done_o.at[:, cols], out.at[:, cols], flush.at[p, 0]))
        moves.append(pltpu.make_async_copy(done_q.at[:, cols], dq.at[:, cols], flush.at[p, 1]))
    cols = pl.ds(0, EARLY_KV)
    moves.append(pltpu.make_async_copy(done_k, dk.at[:, cols], flush.at[pieces, 0]))
    moves.append(pltpu.make_async_copy(done_v, dv.at[:, cols], flush.at[pieces, 1]))
    for move in moves:
        move.start()

    def one(n, first):
        return first + jnp.where(owners[n] < me, lens[n], 0)

    shift = lax.fori_loop(0, lens.shape[0], one, jnp.int32(0)) - (me * TOK - HALO)
    shift = jnp.clip(shift, 0, 2 * HALO)
    middle = slice(HALO, HALO + TOK)
    for ref, part in ((out_tall, out_part), (dq_tall, dq_part)):
        ref[:, middle, :] = part[:, middle, :]
    clear((out_tall, dq_tall))
    dk_tall[...] = dk_part[...]
    dv_tall[...] = dv_part[...]
    n = KV_HEADS - 1
    halo_pass(
        False, last_q, last_g, head_rows(kw, n), head_rows(vw, n), (None, None, bias_after), owned,
        out_tall, dq_tall, dk_tall, dv_tall, parcel,
    )
    shift_queries(shift, out_tall, dq_tall, stage_o, stage_q)
    shift_keys(shift, dk_tall, dv_tall, stage_k, stage_v)
    cols = pl.ds(EARLY_COLS, LAST_COLS)
    rest = [
        pltpu.make_async_copy(stage_o, out.at[:, cols], store.at[0]),
        pltpu.make_async_copy(stage_q, dq.at[:, cols], store.at[1]),
        pltpu.make_async_copy(stage_k, dk.at[:, kv_cols(n)], store.at[2]),
        pltpu.make_async_copy(stage_v, dv.at[:, kv_cols(n)], store.at[3]),
    ]
    for move in rest:
        move.start()
    for move in moves + rest:
        move.wait()


def local(devices, q, k, v, g, lens, owners, table):
    any_spec = pl.BlockSpec(memory_space=pl.ANY)
    vmem = pl.BlockSpec(memory_space=pltpu.VMEM)
    smem = pl.BlockSpec(memory_space=pltpu.SMEM)
    q, k, v, g, lens, owners, table = [
        pltpu.with_memory_space_constraint(x, pltpu.HBM) for x in (q, k, v, g, lens, owners, table)
    ]
    def tall(count):
        return pltpu.VMEM((count, TALL, HEAD_DIM), F32)

    def bias(b):
        return pltpu.VMEM((BLOCKS[b][3] - BLOCKS[b][2], CW), F32)

    def lent(u):
        return pltpu.VMEM((HALO, 2 * HALO * UNITS[u][2] + 2 * HEAD_DIM), BF16)

    kv_tall = pltpu.VMEM((TALL, HEAD_DIM), F32)
    units = len(UNITS)
    last_talls = [tall(UNITS[-1][2])] * 2 + [kv_tall] * 2
    mid_shapes = (
        [pltpu.VMEM((WIN, KV_COLS), BF16)] * 2
        + [bias(AFTER), pltpu.VMEM((len(BLOCKS), 8, CW), F32)]
        + [pltpu.VMEM((WIN, LAST_COLS), BF16)] * 2
        + [pltpu.VMEM((CAP, EARLY_COLS), BF16)] * 2
        + [pltpu.VMEM((CAP, EARLY_KV), BF16)] * 2
        + last_talls
        + [lent(units - 1)]
    )
    near = [pltpu.VMEM((WIN, count * HEAD_DIM), BF16) for _, _, count in UNITS[:-1] for _ in range(2)]
    talls = [tall(count) for _, _, count in UNITS[:-1] for _ in range(2)]
    dma = pltpu.SemaphoreType.DMA
    mid = pl.pallas_call(
        functools.partial(exchange_kernel, devices),
        out_shape=mid_shapes,
        in_specs=[any_spec] * 4 + [smem] * 3,
        out_specs=[vmem] * len(mid_shapes),
        scratch_shapes=[bias(0), bias(1), bias(LENT)]
        + near
        + talls
        + [kv_tall] * (2 * (KV_HEADS - 1))
        + [lent(u) for u in range(units - 1)]
        + [lent(u) for u in range(units)]
        + [pltpu.VMEM((HALO, UNITS[u][2] * HEAD_DIM), BF16) for _ in range(2) for u in RELAYED for _ in range(2)]
        + [dma((units, 2))] * 3
        + [dma((2, 2))] * 2
        + [dma((2,))]
        + [dma((units,))] * 2
        + [dma((3, len(RELAYED), 2))] * 2,
        compiler_params=pltpu.CompilerParams(
            collective_id=0, has_side_effects=True, vmem_limit_bytes=40 << 20
        ),
        name="exchange",
    )(q, g, k, v, lens, owners, table)
    mid = [pltpu.with_memory_space_constraint(x, pltpu.VMEM) for x in mid]
    shapes = [(CAP, w) for w in (HEADS * HEAD_DIM,) * 2 + (KV_COLS,) * 2]
    return tuple(
        pl.pallas_call(
            finish_kernel,
            out_shape=[pltpu.HBM(s, BF16) for s in shapes],
            in_specs=[smem] * 2 + [vmem] * len(mid),
            out_specs=[any_spec] * 4,
            scratch_shapes=[pltpu.VMEM((CAP, LAST_COLS), BF16)] * 2
            + [pltpu.VMEM((CAP, HEAD_DIM), BF16)] * 2
            + last_talls
            + [dma((3, 2)), dma((4,))],
            compiler_params=pltpu.CompilerParams(vmem_limit_bytes=24 << 20),
            name="finish",
        )(lens, owners, *mid)
    )


def solution(mesh):
    rows = P(("dp", "seq"), None)
    return jax.shard_map(
        functools.partial(local, mesh.shape["seq"]),
        mesh=mesh,
        in_specs=(rows, rows, rows, rows, P("dp"), P("dp"), P("dp", None)),
        out_specs=(rows, rows, rows, rows),
        check_vma=False,
    )
```
